256 devices in a mesh: pair: 16 (over y, x), blk: 8 (over z), rep: 2 (over core).
Axes of the slice: x: 4, y: 4, z: 8, core: 2. Of those that a mesh axis runs over, the one named last changes fastest.
Arguments:
- amplitudes: float32 [12, 80, 608, 608], P(None, ('blk', 'rep'), None, 'pair'), may hold values from -6 to 6
- integrals: float32 [80, 608, 1, 608], P(('blk', 'rep')), may hold values from -0.0390625 to 0.0390625
- virt_sizes: int32 [8], replicated, may hold values from 1 to 152, 608 in all
- i_irrep: int32 [12], replicated, may hold values from 0 to 7
- j_irrep: int32 [1], replicated, may hold values from 0 to 7
Outputs:
- residual: float32 [12, 608, 1, 608], P(None, 'pair', None, ('blk', 'rep'))
The draws below stay inside these ranges and needn't reach their ends.
Inputs may be any that keep to these rules, and one draw needn't show every extreme that they name: `virt_sizes`: the entries sum to 608.
All inputs are finite; a program needn't handle non-finite values.
Results may differ from the reference program's by a relative error of at most 0.00016.
Values sent between devices are 32-bit elements; how exact they have to be, the bound alone decides.
No kernel may reach another device: no remote copies, remote signals or barrier semaphores. Data moves between devices by JAX's collectives and lax.ppermute only.
A program may use at most 128 MiB of HBM per device.

```python
import math
import jax
import jax.numpy as jnp
import numpy as np
from jax import lax

OCC = 80
V = 608
IRREPS = 8
NI = 12
NJ = 1


def set_ends(array, stream_key, least, high):
    place = [jax.random.randint(jax.random.fold_in(stream_key, axis), (), 0, length) for axis, length in enumerate(array.shape)]
    widest = array.shape.index(max(array.shape))
    beside = place[:widest] + [(place[widest] + 1) % array.shape[widest]] + place[widest + 1:]
    return array.at[tuple(place)].set(least).at[tuple(beside)].set(high)


def strengthened(array, rng, source, target, parts, factor):
    def block_of(axis_at):
        return (jnp.arange(array.shape[axis_at]) // (array.shape[axis_at] // parts)).reshape((-1,) + (1,) * (array.ndim - 1 - axis_at))

    first = jax.random.permutation(rng, parts)[block_of(target)]
    far = (block_of(target) + parts // 2) % parts
    return jnp.where((block_of(source) == first) | (block_of(source) == far), factor * array, array)


def level_of(rng, shape, cuts, low, largest):
    factor_of = 1.0
    for dim, parts in cuts:
        draws = jax.random.uniform(jax.random.fold_in(jax.random.fold_in(rng, 6), dim), (parts,), jnp.float32, low / len(cuts), largest / len(cuts))
        factor_of = factor_of * jnp.repeat(jnp.exp(draws), shape[dim] // parts).reshape((-1,) + (1,) * (len(shape) - 1 - dim))
    return factor_of


def profile(number_of, total, bound, lean):
    weights = [(1 << 20) // math.isqrt(rank ** lean) + 1 for rank in range(2, number_of + 1)]
    spare, given = total - bound - (number_of - 1), [1] * (number_of - 1)
    while spare > 0:
        movable = [i for i in range(number_of - 1) if given[i] < bound]
        pool, left = sum([weights[i] for i in movable]), spare
        for i in movable:
            addition = min(bound - given[i], max(1, left * weights[i] // pool), spare)
            given[i] = given[i] + addition
            spare = spare - addition
    return np.array([bound] + given)


def ragged_sizes(rng, amount, total, limit, lean):
    if amount == 2:
        one = jax.random.randint(rng, (), max(1, total - limit), min(limit, total - 1) + 1)
        return jnp.stack([one, total - one])
    lengths = jnp.asarray(profile(amount, total, limit, lean), jnp.int32)
    pairs = (amount - 1) // 2
    source_of, sink = lengths[1:1 + 2 * pairs:2], lengths[2:2 + 2 * pairs:2]
    room = jnp.minimum(source_of - 1, limit - sink)
    moved = jax.random.randint(jax.random.fold_in(rng, 1), (pairs,), 0, 1 << 20) % (room + 1)
    lengths = lengths.at[1:1 + 2 * pairs:2].set(source_of - moved).at[2:2 + 2 * pairs:2].set(sink + moved)
    return lengths[jax.random.permutation(jax.random.fold_in(rng, 2), amount)]


def gaussian(rng, shape, width, bound, split=(), held_as=jnp.bfloat16):
    factor_of = level_of(rng, shape, split, -0.22, 0.18) if split else 1.0
    values = jax.random.normal(rng, shape, jnp.float32) * width * factor_of
    return jnp.minimum(jnp.maximum(values, -bound), bound).astype(held_as)


def bell_draw_with(own_key, extent, spread, bound, pieces, heavy, kind=jnp.bfloat16):
    result = spread * jax.random.normal(own_key, extent, jnp.float32)
    if pieces:
        result = result * level_of(own_key, extent, pieces, -0.22, 0.18)
    return jnp.clip(strengthened(result, jax.random.fold_in(own_key, 3), *heavy), -bound, bound).astype(kind)


def setup_inputs(seed: int = 0) -> dict:
    seeds = jax.random.split(jax.random.key(seed), 6)
    amplitudes = gaussian(seeds[0], (NI, OCC, V, V), 1.0, 6.0, ((1, 16), (3, 16)), jnp.float32)
    integrals = bell_draw_with(seeds[1], (OCC, V, NJ, V), (OCC * V) ** -0.5, 0.0390625, ((0, 16),), (0, 3, 16, 2.0), jnp.float32)
    virt_sizes = ragged_sizes(seeds[2], IRREPS, V, V // 4, 2).astype(jnp.int32)
    i_irrep = set_ends(jax.random.randint(seeds[3], (NI,), 0, IRREPS), jax.random.fold_in(seeds[3], 1), 0, IRREPS - 1).astype(jnp.int32)
    j_irrep = jax.random.randint(seeds[4], (NJ,), 0, IRREPS).astype(jnp.int32)
    return dict(amplitudes=amplitudes, integrals=integrals, virt_sizes=virt_sizes, i_irrep=i_irrep, j_irrep=j_irrep)


def virt_irreps(virt_sizes, count):
    ends = jnp.cumsum(virt_sizes).astype(jnp.int32)
    index = jnp.arange(count, dtype=jnp.int32)
    return jnp.sum((index[:, None] >= ends[None, :]).astype(jnp.int32), axis=1).astype(jnp.int32)


def reference(amplitudes, integrals, virt_sizes, i_irrep, j_irrep):
    def one_row(block):
        return jnp.einsum("kac,kcjb->ajb", block, integrals, precision=lax.Precision.HIGHEST)

    cycle = lax.map(one_row, amplitudes)
    irreps = virt_irreps(virt_sizes, V)
    left = jnp.bitwise_xor(i_irrep[:, None], irreps[None, :])
    right = jnp.bitwise_xor(j_irrep[:, None], irreps[None, :])
    keep = left[:, :, None, None] == right[None, None, :, :]
    return jnp.where(keep, cycle, jnp.float32(0.0))
```

```python
import functools

import jax
import jax.numpy as jnp
from jax import lax
from jax.experimental import pallas as pl
from jax.experimental.pallas import tpu as pltpu
from jax.sharding import PartitionSpec as P

NI, KL, CL, V, G = 12, 5, 38, 608, 8
PAIR, BLK = 16, 8
KP = 208
WIN = 80
SEG = 360
IG = 3
NIG = NI // IG
LANES = 128
ROWS = 40
F32, BF16, I32 = jnp.float32, jnp.bfloat16, jnp.int32
SMEM = pl.BlockSpec(memory_space=pltpu.SMEM)
VM = pl.BlockSpec(memory_space=pltpu.VMEM)
PARAMS = pltpu.CompilerParams(vmem_limit_bytes=40 * 1024 * 1024)


def ends_of(sizes):
    ends, total = [], jnp.int32(0)
    for g in range(G):
        total = total + sizes[g]
        ends.append(total)
    return ends


def below(x, r):
    full = (x * 863) >> 16
    return 38 * full + jnp.clip(x - 76 * full - 38 * r, 0, 38)


def groups_of(ends, r):
    first, number, offset = [], [], []
    last, row = jnp.int32(0), jnp.int32(0)
    for g in range(G):
        here = below(ends[g], r)
        first.append(last)
        number.append(here - last)
        offset.append(row)
        row = row + (((here - last) + 7) >> 3) * 8
        last = here
    return first, number, offset


def lane_target(ends, ii, jj, ig, p):
    lane = lax.broadcasted_iota(I32, (1, LANES), 1)
    second, third = lane >= 38, lane >= 76
    a = 38 * p + lane - jnp.where(third, 76, jnp.where(second, 38, 0))
    irrep = jnp.zeros((1, LANES), I32)
    for g in range(G):
        irrep = irrep + (a >= ends[g]).astype(I32)
    j = jj[0]
    h = jnp.where(third, ii[IG * ig + 2] ^ j, jnp.where(second, ii[IG * ig + 1] ^ j, ii[IG * ig] ^ j))
    return irrep ^ h


def split(x):
    hi = x.astype(BF16)
    return hi, (x - hi.astype(F32)).astype(BF16)


def prep_kernel(meta, sizes, w_ref, out_ref, wk):
    r = meta[2]
    wk[...] = jnp.zeros_like(wk)
    for k in range(KL):
        wk[40 * k:40 * k + CL, :] = w_ref[k]
    ends = ends_of(sizes)
    hi, lo = split(wk[...])
    nt = (((1,), (1,)), ((), ()))
    for seg in range(2):
        rs = r ^ seg
        first, number, offset = groups_of(ends, rs)
        row = lax.broadcasted_iota(I32, (SEG, 1), 0)
        bp = jnp.full((SEG, 1), -1, I32)
        for g in range(G):
            inside = (row >= offset[g]) & (row < offset[g] + number[g])
            bp = jnp.where(inside, row - offset[g] + first[g], bp)
        b = jnp.where(bp < 0, -1, bp + 38 * ((bp * 1725) >> 16) + 38 * rs)
        pick = (lax.broadcasted_iota(I32, (SEG, V), 1) == b).astype(F32).astype(BF16)
        rows = slice(seg * SEG, (seg + 1) * SEG)
        wh = lax.dot_general(pick, hi, nt, preferred_element_type=F32).astype(BF16)
        wl = lax.dot_general(pick, lo, nt, preferred_element_type=F32).astype(BF16)
        out_ref[rows, 0:KP] = wh
        out_ref[rows, KP:2 * KP] = wh
        out_ref[rows, 2 * KP:3 * KP] = wl


def prep(meta, sizes, w):
    return pl.pallas_call(
        prep_kernel,
        out_shape=jax.ShapeDtypeStruct((2 * SEG, 3 * KP), BF16),
        in_specs=[SMEM, SMEM, VM],
        out_specs=VM,
        scratch_shapes=[pltpu.VMEM((KP, V), F32)],
        compiler_params=PARAMS,
    )(meta, sizes, w)


def main_kernel(ig0, xfirst, meta, sizes, ii, jj, w_ref, t_ref, own_ref, oth_ref, x, t_all, d):
    me, r = meta[0], meta[2]
    ig = ig0 + pl.program_id(0)

    @pl.when(pl.program_id(0) == 0)
    def _():
        x[...] = jnp.zeros_like(x)
        d[2 * SEG:, :] = jnp.zeros((WIN, 2 * LANES), F32)

    for p in range(PAIR):
        at = LANES * (p % 2)
        for k in range(KL):
            parts = [t_ref[i, k, :, 38 * p:38 * p + 38] for i in range(IG)]
            parts.append(jnp.zeros((CL, LANES - 38 * IG), F32))
            x[40 * k:40 * k + CL, at:at + LANES] = jnp.concatenate(parts, axis=1)
        if p % 2:
            hi, lo = split(x[...])
            t_all[p // 2, 0:KP, :] = hi
            t_all[p // 2, KP:2 * KP, :] = lo
            t_all[p // 2, 2 * KP:3 * KP, :] = hi

    ends = ends_of(sizes)
    offsets = [groups_of(ends, r ^ seg)[2] for seg in range(2)]

    def body(q, carry):
        d[0:2 * SEG, :] = jnp.dot(w_ref[...], t_all[q], preferred_element_type=F32)
        for half in range(2):
            p = 2 * q + half
            target = lane_target(ends, ii, jj, ig, p)
            rel = p ^ me
            place = (rel & 3) * 4 + (rel >> 2) if xfirst else rel
            for seg, ref in ((0, own_ref), (1, oth_ref)):
                acc = jnp.zeros((WIN, LANES), F32)
                for g in range(G):
                    start = pl.multiple_of(seg * SEG + offsets[seg][g], 8)
                    acc = jnp.where(target == g, d[pl.ds(start, WIN), half * LANES:(half + 1) * LANES], acc)
                ref[0, place] = acc
        return carry

    lax.fori_loop(0, PAIR // 2, body, 0)


def main(ig0, n, xfirst, meta, sizes, ii, jj, w, t):
    packed = jax.ShapeDtypeStruct((n, PAIR, WIN, LANES), F32)
    block = pl.BlockSpec((1, PAIR, WIN, LANES), lambda s: (s, 0, 0, 0))
    return pl.pallas_call(
        functools.partial(main_kernel, ig0, xfirst),
        out_shape=(packed, packed),
        grid=(n,),
        in_specs=[SMEM, SMEM, SMEM, SMEM, pl.BlockSpec((2 * SEG, 3 * KP), lambda s: (0, 0)),
                  pl.BlockSpec((IG, KL, CL, V), lambda s: (ig0 + s, 0, 0, 0))],
        out_specs=(block, block),
        scratch_shapes=[pltpu.VMEM((KP, 2 * LANES), F32), pltpu.VMEM((PAIR // 2, 3 * KP, 2 * LANES), BF16),
                        pltpu.VMEM((2 * SEG + WIN, 2 * LANES), F32)],
        compiler_params=PARAMS,
        cost_estimate=pl.CostEstimate(flops=n * 2 * 720 * 624 * 2048, bytes_accessed=n * 3000000, transcendentals=0),
    )(meta, sizes, ii, jj, w, t)


def add_kernel(a_ref, b_ref, *outs):
    for d in range(4):
        outs[d][0, 0] = a_ref[0, d, 0] + b_ref[0, d, 0]


def add_parts(a, b):
    n = a.shape[0]
    a, b = (v.reshape(n, 4, 4, WIN, LANES) for v in (a, b))
    block = pl.BlockSpec((1, 4, 1, WIN, LANES), lambda s, u: (s, 0, u, 0, 0))
    return pl.pallas_call(
        add_kernel,
        out_shape=[jax.ShapeDtypeStruct((n, 4, WIN, LANES), F32)] * 4,
        grid=(n, 4),
        in_specs=[block, block],
        out_specs=[pl.BlockSpec((1, 1, WIN, LANES), lambda s, u: (s, u, 0, 0))] * 4,
        compiler_params=PARAMS,
        cost_estimate=pl.CostEstimate(flops=1000000, bytes_accessed=n * 2000000, transcendentals=0),
    )(a, b)


def sum_kernel(*refs):
    ins, outs = refs[:4], refs[4:]
    for u in range(4):
        outs[u][...] = (ins[0][:, u] + ins[1][:, u]) + (ins[2][:, u] + ins[3][:, u])


def sum_parts(parts):
    n = parts[0].shape[0]
    return pl.pallas_call(
        sum_kernel,
        out_shape=[jax.ShapeDtypeStruct((n, WIN, LANES), F32)] * 4,
        in_specs=[VM] * 4,
        out_specs=[VM] * 4,
        compiler_params=PARAMS,
    )(*parts)


def dense_kernel(igs, meta, sizes, ii, jj, *refs):
    a_refs, b_refs, outs, full = refs[:4], refs[4:8], refs[8:16], refs[16]
    me, z, r = meta[0], meta[1], meta[2]
    ends = ends_of(sizes)
    first, number, _ = groups_of(ends, r)
    row = lax.broadcasted_iota(I32, (BLK * ROWS, 1), 0)
    block = (row * 1639) >> 16
    beta = row - ROWS * block
    bp = jnp.where(beta < 38, 38 * block + beta, 400)
    group, base = jnp.full_like(bp, -1), jnp.zeros_like(bp)
    for g in range(G):
        inside = (bp >= first[g]) & (bp < first[g] + number[g])
        group = jnp.where(inside, g, group)
        base = jnp.where(inside, first[g], base)
    window = lax.broadcasted_iota(I32, (BLK * ROWS, WIN), 1)
    pick = ((window == bp - base) & (group >= 0)).astype(F32).astype(BF16)
    for side, part in enumerate((a_refs, b_refs)):
        for s in range(len(igs[side])):
            ig = igs[side][s]
            x = (part[0][s] + part[1][s]) + (part[2][s] + part[3][s])
            hi, mid = split(x)
            lo = ((x - hi.astype(F32)) - mid.astype(F32)).astype(BF16)
            y = jnp.dot(pick, hi, preferred_element_type=F32)
            y = y + jnp.dot(pick, mid, preferred_element_type=F32)
            y = y + jnp.dot(pick, lo, preferred_element_type=F32)
            target = lane_target(ends, ii, jj, ig, me)
            full[:, ig] = jnp.where(group == target, y, 0.0).reshape(BLK, ROWS, LANES)
    for d in range(BLK):
        outs[d][...] = full[z ^ d]


def dense(igs, meta, sizes, ii, jj, a_parts, b_parts):
    return pl.pallas_call(
        functools.partial(dense_kernel, igs),
        out_shape=[jax.ShapeDtypeStruct((NIG, ROWS, LANES), F32)] * BLK,
        in_specs=[SMEM] * 4 + [VM] * 8,
        out_specs=[VM] * BLK,
        scratch_shapes=[pltpu.VMEM((BLK, NIG, ROWS, LANES), F32)],
        compiler_params=PARAMS,
    )(meta, sizes, ii, jj, *a_parts, *b_parts)


def final_kernel(*refs):
    ins, out = refs[:BLK], refs[BLK]
    for ig in range(NIG):
        parts = [ins[d][ig] for d in range(BLK)]
        x = ((parts[0] + parts[1]) + (parts[2] + parts[3])) + ((parts[4] + parts[5]) + (parts[6] + parts[7]))
        y = x.T
        for i in range(IG):
            out[IG * ig + i] = y[38 * i:38 * i + 38, 0:38]


def final(parts):
    return pl.pallas_call(
        final_kernel,
        out_shape=jax.ShapeDtypeStruct((NI, 38, 38), F32),
        in_specs=[VM] * BLK,
        out_specs=VM,
        compiler_params=PARAMS,
    )(*parts)


def exchange(parts, axis, step, size):
    got = [parts[0]]
    for d in range(1, len(parts)):
        got.append(lax.ppermute(parts[d], axis, [(p, p ^ (step * d)) for p in range(size)]))
    return got


def per_device(amplitudes, integrals, virt_sizes, i_irrep, j_irrep):
    p, z, r = lax.axis_index("pair"), lax.axis_index("blk"), lax.axis_index("rep")
    meta = jnp.stack([p, z, r]).astype(I32)
    small = (meta, virt_sizes, i_irrep, j_irrep)
    t = jnp.swapaxes(amplitudes, 2, 3)
    w = lax.dynamic_slice(integrals, (0, CL * p, 0, 0), (KL, CL, 1, V)).reshape(KL, CL, V)
    rows = prep(meta, virt_sizes, w)
    stage = []
    igs = ((0, 1), (2, 3))
    for side in range(2):
        own, other = main(igs[side][0], 2, side == 0, *small, rows, t)
        got = lax.ppermute(other, "rep", [(0, 1), (1, 0)])
        stage.append(add_parts(own, got))
    stage = [exchange(stage[0], "pair", 1, PAIR), exchange(stage[1], "pair", 4, PAIR)]
    stage = [sum_parts(s) for s in stage]
    stage = [exchange(stage[0], "pair", 4, PAIR), exchange(stage[1], "pair", 1, PAIR)]
    parts = dense(igs, *small, *stage)
    out = final(exchange(parts, "blk", 1, BLK))
    return out.reshape(NI, 38, 1, 38)


def solution(mesh):
    return jax.shard_map(
        per_device,
        mesh=mesh,
        in_specs=(
            P(None, ("blk", "rep"), None, "pair"),
            P(("blk", "rep"), None, None, None),
            P(),
            P(),
            P(),
        ),
        out_specs=P(None, "pair", None, ("blk", "rep")),
        check_vma=False,
    )
```

```python
import functools

import jax
import jax.numpy as jnp
from jax import lax
from jax.experimental import pallas as pl
from jax.experimental.pallas import tpu as pltpu
from jax.sharding import PartitionSpec as P

NI, KL, CL, V, G = 12, 5, 38, 608, 8
PAIR, BLK = 16, 8
KP = 208
WIN = 80
SEG = 360
IG = 3
NIG = NI // IG
PARTS = ((0, 1), (2, 3))
LANES = 128
WIDE = 640
CUTS = (0, 192, 384, 560, 720)
USED = 76
F32, BF16, I32 = jnp.float32, jnp.bfloat16, jnp.int32
SMEM = pl.BlockSpec(memory_space=pltpu.SMEM)
VM = pl.BlockSpec(memory_space=pltpu.VMEM)
PARAMS = pltpu.CompilerParams(vmem_limit_bytes=16 * 1024 * 1024)
LARGE = pltpu.CompilerParams(vmem_limit_bytes=48 * 1024 * 1024)


def ends_of(sizes):
    ends, total = [], jnp.int32(0)
    for g in range(G):
        total = total + sizes[g]
        ends.append(total)
    return ends


def below(x, r):
    full = (x * 863) >> 16
    return 38 * full + jnp.clip(x - 76 * full - 38 * r, 0, 38)


def groups_of(ends, r):
    first, number, offset = [], [], []
    last, row = jnp.int32(0), jnp.int32(0)
    for g in range(G):
        here = below(ends[g], r)
        first.append(last)
        number.append(here - last)
        offset.append(row)
        row = row + (((here - last) + 7) >> 3) * 8
        last = here
    return first, number, offset


def lane_target(ends, ii, jj, ig, p):
    lane = lax.broadcasted_iota(I32, (1, LANES), 1)
    second, third = lane >= 38, lane >= 76
    a = 38 * p + lane - jnp.where(third, 76, jnp.where(second, 38, 0))
    irrep = jnp.zeros((1, LANES), I32)
    for g in range(G):
        irrep = irrep + (a >= ends[g]).astype(I32)
    j = jj[0]
    h = jnp.where(third, ii[IG * ig + 2] ^ j, jnp.where(second, ii[IG * ig + 1] ^ j, ii[IG * ig] ^ j))
    return irrep ^ h


def split(x):
    hi = x.astype(BF16)
    return hi, (x - hi.astype(F32)).astype(BF16)


def window_rows(sizes, r, wk, out_ref):
    ends = ends_of(sizes)
    hi, lo = split(wk[...])
    nt = (((1,), (1,)), ((), ()))
    for seg in range(2):
        rs = r ^ seg
        first, number, offset = groups_of(ends, rs)
        row = lax.broadcasted_iota(I32, (SEG, 1), 0)
        bp = jnp.full((SEG, 1), -1, I32)
        for g in range(G):
            inside = (row >= offset[g]) & (row < offset[g] + number[g])
            bp = jnp.where(inside, row - offset[g] + first[g], bp)
        b = jnp.where(bp < 0, -1, bp + 38 * ((bp * 1725) >> 16) + 38 * rs)
        pick = (lax.broadcasted_iota(I32, (SEG, V), 1) == b).astype(F32).astype(BF16)
        rows = slice(seg * SEG, (seg + 1) * SEG)
        wh = lax.dot_general(pick, hi, nt, preferred_element_type=F32).astype(BF16)
        wl = lax.dot_general(pick, lo, nt, preferred_element_type=F32).astype(BF16)
        out_ref[rows, 0:KP] = wh
        out_ref[rows, KP:2 * KP] = wh
        out_ref[rows, 2 * KP:3 * KP] = wl


def main_kernel(i0, count, first_call, meta, sizes, ii, jj, w_in, t_hbm, *refs):
    if first_call:
        own_ref, oth_ref, rows_ref, raw, wk, raw_sem = refs[:6]
        refs = refs[6:]
    else:
        own_ref, oth_ref = refs[:2]
        rows_ref = w_in
        refs = refs[2:]
    t_buf, x, t_all, d0, d1, in_sem = refs
    r = meta[2]
    loads = [pltpu.make_async_copy(t_hbm.at[i0 + n], t_buf.at[n], in_sem.at[n]) for n in range(count)]
    if first_call:
        at = meta[0] * CL
        raws = [pltpu.make_async_copy(w_in.at[k, pl.ds(at, CL)], raw.at[k], raw_sem.at[k]) for k in range(KL)]
        for c in raws:
            c.start()
    for c in loads:
        c.start()
    x[...] = jnp.zeros_like(x)
    for d in (d0, d1):
        d[2 * SEG:, :] = jnp.zeros((WIN, 2 * LANES), F32)
    if first_call:
        wk[...] = jnp.zeros_like(wk)
        for c in raws:
            c.wait()
        for k in range(KL):
            wk[40 * k:40 * k + CL, :] = raw[k, :, 0, :]
        window_rows(sizes, r, wk, rows_ref)
    ends = ends_of(sizes)
    offsets = [groups_of(ends, r ^ seg)[2] for seg in range(2)]
    lane = lax.broadcasted_iota(I32, (1, WIDE), 1)
    irrep = jnp.zeros((1, WIDE), I32)
    for g in range(G):
        irrep = irrep + (lane >= ends[g]).astype(I32)

    def prepare(n):
        loads[n].wait()
        slot, odd = (n // 2) % 2, n % 2
        for k in range(KL):
            x[n % 2, 40 * k:40 * k + CL, 0:V] = t_buf[n, k]
        for c in range(5):
            tile, half = (2, odd) if c == 4 else (3 * odd + c // 2, c % 2)
            lanes = slice(half * LANES, (half + 1) * LANES)
            hi, lo = split(x[n % 2, :, c * LANES:(c + 1) * LANES])
            t_all[slot, tile, 0:KP, lanes] = hi
            t_all[slot, tile, KP:2 * KP, lanes] = lo
            t_all[slot, tile, 2 * KP:3 * KP, lanes] = hi

    def select(u, half, seg):
        pair, tile = units[u]
        d = (d0, d1)[u % 2]
        if tile == 2:
            n, c = 2 * pair + half, 4
        else:
            n, c = 2 * pair + tile // 3, 2 * (tile % 3) + half
        if n >= count:
            return
        target = irrep[:, c * LANES:(c + 1) * LANES] ^ (ii[i0 + n] ^ jj[0])
        acc = None
        for g in range(G):
            start = pl.multiple_of(seg * SEG + offsets[seg][g], 8)
            part = d[pl.ds(start, WIN), half * LANES:(half + 1) * LANES]
            acc = part if g == 0 else jnp.where(target == g, part, acc)
        (own_ref, oth_ref)[seg][n, :, c * LANES:(c + 1) * LANES] = acc

    units = [divmod(u, 5) for u in range(5 * (count // 2) + 3 * (count % 2))]
    prepare(0)
    prepare(1)
    pieces = [(half, seg) for half in range(2) for seg in range(2)]
    for u in range(len(units)):
        pair, tile = units[u]
        for m, (half, seg) in enumerate(pieces):
            rows = slice(CUTS[m], CUTS[m + 1])
            (d0, d1)[u % 2][rows, :] = jnp.dot(rows_ref[rows, :], t_all[pair % 2, tile], preferred_element_type=F32)
            if u:
                select(u - 1, half, seg)
        if tile in (0, 2) and 2 * pair + 2 + tile // 2 < count:
            prepare(2 * pair + 2 + tile // 2)
    for half, seg in pieces:
        select(len(units) - 1, half, seg)


def main(i0, count, meta, sizes, ii, jj, w, t, first_call):
    packed = jax.ShapeDtypeStruct((count, WIN, WIDE), F32)
    rows = jax.ShapeDtypeStruct((2 * SEG, 3 * KP), BF16)
    hbm = pl.BlockSpec(memory_space=pl.ANY)
    extra = [pltpu.VMEM((KL, CL, 1, V), F32), pltpu.VMEM((KP, V), F32), pltpu.SemaphoreType.DMA((KL,))]
    return pl.pallas_call(
        functools.partial(main_kernel, i0, count, first_call),
        out_shape=(packed, packed, rows) if first_call else (packed, packed),
        in_specs=[SMEM, SMEM, SMEM, SMEM, hbm if first_call else VM, hbm],
        out_specs=(VM, VM, VM) if first_call else (VM, VM),
        scratch_shapes=(extra if first_call else []) + [
            pltpu.VMEM((count, KL, CL, V), F32),
            pltpu.VMEM((2, KP, WIDE), F32),
            pltpu.VMEM((2, 5, 3 * KP, 2 * LANES), BF16),
            pltpu.VMEM((2 * SEG + WIN, 2 * LANES), F32),
            pltpu.VMEM((2 * SEG + WIN, 2 * LANES), F32),
            pltpu.SemaphoreType.DMA((count,)),
        ],
        compiler_params=LARGE,
        cost_estimate=pl.CostEstimate(flops=count * 1000000000, bytes_accessed=count * 1000000, transcendentals=0),
    )(meta, sizes, ii, jj, w, t)


def add_kernel(xfirst, meta, own_ref, got_ref, *refs):
    outs, total, tiles = refs[:4], refs[4], refs[5]
    me = meta[0]
    total[...] = own_ref[...] + got_ref[...]
    for p in range(PAIR):
        rel = p ^ me
        low, high = rel & 3, rel >> 2
        d, u = (low, high) if xfirst else (high, low)
        for s in range(own_ref.shape[0] // IG):
            parts = [total[IG * s + i, 0:USED, 38 * p:38 * p + 38] for i in range(IG)]
            parts.append(jnp.zeros((USED, LANES - 38 * IG), F32))
            tiles[d, u, USED * s:USED * (s + 1), :] = jnp.concatenate(parts, axis=1)
    for d in range(4):
        outs[d][...] = tiles[d]


def add_parts(xfirst, meta, own, got):
    rows = own.shape[0] // IG * USED
    return pl.pallas_call(
        functools.partial(add_kernel, xfirst),
        out_shape=[jax.ShapeDtypeStruct((4, rows, LANES), F32)] * 4,
        in_specs=[SMEM, VM, VM],
        out_specs=[VM] * 4,
        scratch_shapes=[pltpu.VMEM(own.shape, F32), pltpu.VMEM((4, 4, rows, LANES), F32)],
        compiler_params=PARAMS,
        cost_estimate=pl.CostEstimate(flops=1, bytes_accessed=1, transcendentals=0),
    )(meta, own, got)


def sum_kernel(*refs):
    ins, outs = refs[:4], refs[4:]
    for u in range(4):
        outs[u][...] = (ins[0][u] + ins[1][u]) + (ins[2][u] + ins[3][u])


def sum_parts(parts):
    rows = parts[0].shape[1]
    return pl.pallas_call(
        sum_kernel,
        out_shape=[jax.ShapeDtypeStruct((rows, LANES), F32)] * 4,
        in_specs=[VM] * 4,
        out_specs=[VM] * 4,
        compiler_params=PARAMS,
    )(*parts)


def dense_kernel(meta, sizes, ii, jj, *refs):
    sides, outs, full = (refs[:4], refs[4:8]), refs[8:16], refs[16]
    me, z, r = meta[0], meta[1], meta[2]
    ends = ends_of(sizes)
    first, number, _ = groups_of(ends, r)
    bp = lax.broadcasted_iota(I32, (BLK * CL, 1), 0)
    group, base = jnp.full_like(bp, -1), jnp.zeros_like(bp)
    for g in range(G):
        inside = (bp >= first[g]) & (bp < first[g] + number[g])
        group = jnp.where(inside, g, group)
        base = jnp.where(inside, first[g], base)
    for side, part in enumerate(sides):
        x = (part[0][...] + part[1][...]) + (part[2][...] + part[3][...])
        hi, mid = split(x)
        lo = ((x - hi.astype(F32)) - mid.astype(F32)).astype(BF16)
        window = lax.broadcasted_iota(I32, (BLK * CL, x.shape[0]), 1)
        for s, ig in enumerate(PARTS[side]):
            pick = (window == bp - base + USED * s).astype(F32).astype(BF16)
            y = jnp.dot(pick, hi, preferred_element_type=F32)
            y = y + jnp.dot(pick, mid, preferred_element_type=F32)
            y = y + jnp.dot(pick, lo, preferred_element_type=F32)
            y = jnp.where(group == lane_target(ends, ii, jj, ig, me), y, 0.0)
            for b in range(BLK):
                full[b, CL * ig:CL * (ig + 1), :] = y[CL * b:CL * (b + 1), :]
    for d in range(BLK):
        outs[d][...] = full[z ^ d]


def dense(meta, sizes, ii, jj, a_parts, b_parts):
    return pl.pallas_call(
        dense_kernel,
        out_shape=[jax.ShapeDtypeStruct((NIG * CL, LANES), F32)] * BLK,
        in_specs=[SMEM] * 4 + [VM] * 8,
        out_specs=[VM] * BLK,
        scratch_shapes=[pltpu.VMEM((BLK, NIG * CL, LANES), F32)],
        compiler_params=PARAMS,
    )(meta, sizes, ii, jj, *a_parts, *b_parts)


def final_kernel(*refs):
    ins, out = refs[:BLK], refs[BLK]
    for ig in range(NIG):
        parts = [ins[d][CL * ig:CL * (ig + 1), :] for d in range(BLK)]
        x = ((parts[0] + parts[1]) + (parts[2] + parts[3])) + ((parts[4] + parts[5]) + (parts[6] + parts[7]))
        y = x.T
        for i in range(IG):
            out[IG * ig + i] = y[38 * i:38 * i + 38, :]


def final(parts):
    return pl.pallas_call(
        final_kernel,
        out_shape=jax.ShapeDtypeStruct((NI, CL, CL), F32),
        in_specs=[VM] * BLK,
        out_specs=VM,
        compiler_params=PARAMS,
    )(*parts)


def exchange(parts, axis, step, size):
    got = [parts[0]]
    for d in range(1, len(parts)):
        got.append(lax.ppermute(parts[d], axis, [(p, p ^ (step * d)) for p in range(size)]))
    return got


def per_device(amplitudes, integrals, virt_sizes, i_irrep, j_irrep):
    p, z, r = lax.axis_index("pair"), lax.axis_index("blk"), lax.axis_index("rep")
    meta = jnp.stack([p, z, r]).astype(I32)
    small = (meta, virt_sizes, i_irrep, j_irrep)
    t = jnp.swapaxes(amplitudes, 2, 3)
    swap = [(0, 1), (1, 0)]
    first, second = (IG * len(part) for part in PARTS)
    own, other, rows = main(0, first, *small, integrals, t, True)
    stage = [add_parts(True, meta, own, lax.ppermute(other, "rep", swap))]
    own, other = main(first, second, *small, rows, t, False)
    stage.append(add_parts(False, meta, own, lax.ppermute(other, "rep", swap)))
    stage = [exchange(stage[0], "pair", 1, PAIR), exchange(stage[1], "pair", 4, PAIR)]
    stage = [sum_parts(s) for s in stage]
    stage = [exchange(stage[0], "pair", 4, PAIR), exchange(stage[1], "pair", 1, PAIR)]
    parts = dense(*small, *stage)
    out = final(exchange(parts, "blk", 1, BLK))
    return out.reshape(NI, 38, 1, 38)


def solution(mesh):
    return jax.shard_map(
        per_device,
        mesh=mesh,
        in_specs=(
            P(None, ("blk", "rep"), None, "pair"),
            P(("blk", "rep"), None, None, None),
            P(),
            P(),
            P(),
        ),
        out_specs=P(None, "pair", None, ("blk", "rep")),
        check_vma=False,
    )
```

```python
import functools

import jax
import jax.numpy as jnp
from jax import lax
from jax.experimental import pallas as pl
from jax.experimental.pallas import tpu as pltpu
from jax.sharding import PartitionSpec as P

NI, KL, CL, V, G = 12, 5, 38, 608, 8
PAIR, BLK = 16, 8
KP = 208
WIN = 80
SEG = 360
IG = 3
NIG = NI // IG
PARTS = ((0, 1), (2, 3))
LANES = 128
WIDE = 640
CUTS = (0, 192, 384, 560, 720)
USED = 76
F32, BF16, I32 = jnp.float32, jnp.bfloat16, jnp.int32
SMEM = pl.BlockSpec(memory_space=pltpu.SMEM)
VM = pl.BlockSpec(memory_space=pltpu.VMEM)
PARAMS = pltpu.CompilerParams(vmem_limit_bytes=16 * 1024 * 1024)
LARGE = pltpu.CompilerParams(vmem_limit_bytes=48 * 1024 * 1024)


def ends_of(info):
    ends, total = [], jnp.int32(0)
    for g in range(G):
        total = total + info[3 + g]
        ends.append(total)
    return ends


def below(x, r):
    full = (x * 863) >> 16
    return 38 * full + jnp.clip(x - 76 * full - 38 * r, 0, 38)


def groups_of(ends, r):
    first, number, offset = [], [], []
    last, row = jnp.int32(0), jnp.int32(0)
    for g in range(G):
        here = below(ends[g], r)
        first.append(last)
        number.append(here - last)
        offset.append(row)
        row = row + (((here - last) + 7) >> 3) * 8
        last = here
    return first, number, offset


def flip_of(info, i):
    return info[11 + i] ^ info[23]


def lane_target(ends, info, ig, p):
    lane = lax.broadcasted_iota(I32, (1, LANES), 1)
    second, third = lane >= 38, lane >= 76
    a = 38 * p + lane - jnp.where(third, 76, jnp.where(second, 38, 0))
    irrep = jnp.zeros((1, LANES), I32)
    for g in range(G):
        irrep = irrep + (a >= ends[g]).astype(I32)
    h = [flip_of(info, IG * ig + i) for i in range(IG)]
    h = jnp.where(third, h[2], jnp.where(second, h[1], h[0]))
    return irrep ^ h


def split(x):
    hi = x.astype(BF16)
    return hi, (x - hi.astype(F32)).astype(BF16)


def window_rows(info, r, wk, out_ref):
    ends = ends_of(info)
    hi, lo = split(wk[...])
    nt = (((1,), (1,)), ((), ()))
    for seg in range(2):
        rs = r ^ seg
        first, number, offset = groups_of(ends, rs)
        row = lax.broadcasted_iota(I32, (SEG, 1), 0)
        bp = jnp.full((SEG, 1), -1, I32)
        for g in range(G):
            inside = (row >= offset[g]) & (row < offset[g] + number[g])
            bp = jnp.where(inside, row - offset[g] + first[g], bp)
        b = jnp.where(bp < 0, -1, bp + 38 * ((bp * 1725) >> 16) + 38 * rs)
        pick = (lax.broadcasted_iota(I32, (SEG, V), 1) == b).astype(F32).astype(BF16)
        rows = slice(seg * SEG, (seg + 1) * SEG)
        wh = lax.dot_general(pick, hi, nt, preferred_element_type=F32).astype(BF16)
        wl = lax.dot_general(pick, lo, nt, preferred_element_type=F32).astype(BF16)
        out_ref[rows, 0:KP] = wh
        out_ref[rows, KP:2 * KP] = wh
        out_ref[rows, 2 * KP:3 * KP] = wl


def main_kernel(info, w_hbm, t_hbm, own_ref, oth_ref, rows_ref, raw, wk, raw_sem, t_buf, x, t_all, d0, d1, in_sem):
    r = info[2]
    at = info[0] * CL
    raws = [pltpu.make_async_copy(w_hbm.at[k, pl.ds(at, CL)], raw.at[k], raw_sem.at[k]) for k in range(KL)]
    loads = [pltpu.make_async_copy(t_hbm.at[n], t_buf.at[n], in_sem.at[n]) for n in range(NI)]
    for c in raws + loads:
        c.start()
    x[...] = jnp.zeros_like(x)
    for d in (d0, d1):
        d[2 * SEG:, :] = jnp.zeros((WIN, 2 * LANES), F32)
    wk[...] = jnp.zeros_like(wk)
    for c in raws:
        c.wait()
    for k in range(KL):
        wk[40 * k:40 * k + CL, :] = raw[k, :, 0, :]
    window_rows(info, r, wk, rows_ref)
    ends = ends_of(info)
    offsets = [groups_of(ends, r ^ seg)[2] for seg in range(2)]
    lane = lax.broadcasted_iota(I32, (1, WIDE), 1)
    irrep = jnp.zeros((1, WIDE), I32)
    for g in range(G):
        irrep = irrep + (lane >= ends[g]).astype(I32)

    def prepare(n):
        loads[n].wait()
        slot, odd = (n // 2) % 2, n % 2
        for k in range(KL):
            x[n % 2, 40 * k:40 * k + CL, 0:V] = t_buf[n, k]
        for c in range(5):
            tile, half = (2, odd) if c == 4 else (3 * odd + c // 2, c % 2)
            lanes = slice(half * LANES, (half + 1) * LANES)
            hi, lo = split(x[n % 2, :, c * LANES:(c + 1) * LANES])
            t_all[slot, tile, 0:KP, lanes] = hi
            t_all[slot, tile, KP:2 * KP, lanes] = lo
            t_all[slot, tile, 2 * KP:3 * KP, lanes] = hi

    def select(u, half, seg):
        pair, tile = units[u]
        d = (d0, d1)[u % 2]
        if tile == 2:
            n, c = 2 * pair + half, 4
        else:
            n, c = 2 * pair + tile // 3, 2 * (tile % 3) + half
        target = irrep[:, c * LANES:(c + 1) * LANES] ^ flip_of(info, n)
        acc = None
        for g in range(G):
            start = pl.multiple_of(seg * SEG + offsets[seg][g], 8)
            part = d[pl.ds(start, WIN), half * LANES:(half + 1) * LANES]
            acc = part if g == 0 else jnp.where(target == g, part, acc)
        (own_ref, oth_ref)[seg][n, :, c * LANES:(c + 1) * LANES] = acc

    units = [divmod(u, 5) for u in range(5 * NI // 2)]
    prepare(0)
    prepare(1)
    pieces = [(half, seg) for half in range(2) for seg in range(2)]
    for u in range(len(units)):
        pair, tile = units[u]
        for m, (half, seg) in enumerate(pieces):
            rows = slice(CUTS[m], CUTS[m + 1])
            (d0, d1)[u % 2][rows, :] = jnp.dot(rows_ref[rows, :], t_all[pair % 2, tile], preferred_element_type=F32)
            if u:
                select(u - 1, half, seg)
        if tile in (0, 2) and 2 * pair + 2 < NI:
            prepare(2 * pair + 2 + tile // 2)
    for half, seg in pieces:
        select(len(units) - 1, half, seg)


def main(info, w, t):
    packed = jax.ShapeDtypeStruct((NI, WIN, WIDE), F32)
    hbm = pl.BlockSpec(memory_space=pl.ANY)
    return pl.pallas_call(
        main_kernel,
        out_shape=(packed, packed),
        in_specs=[SMEM, hbm, hbm],
        out_specs=(VM, VM),
        scratch_shapes=[
            pltpu.VMEM((2 * SEG, 3 * KP), BF16),
            pltpu.VMEM((KL, CL, 1, V), F32),
            pltpu.VMEM((KP, V), F32),
            pltpu.SemaphoreType.DMA((KL,)),
            pltpu.VMEM((NI, KL, CL, V), F32),
            pltpu.VMEM((2, KP, WIDE), F32),
            pltpu.VMEM((2, 5, 3 * KP, 2 * LANES), BF16),
            pltpu.VMEM((2 * SEG + WIN, 2 * LANES), F32),
            pltpu.VMEM((2 * SEG + WIN, 2 * LANES), F32),
            pltpu.SemaphoreType.DMA((NI,)),
        ],
        compiler_params=LARGE,
    )(info, w, t)


def add_kernel(info, own_ref, got_ref, *refs):
    sides, total, tiles = (refs[:4], refs[4:8]), refs[8], refs[9]
    me = info[0]
    total[...] = own_ref[...] + got_ref[...]
    for side, outs in enumerate(sides):
        for p in range(PAIR):
            rel = p ^ me
            low, high = rel & 3, rel >> 2
            d, u = (high, low) if side else (low, high)
            for s, ig in enumerate(PARTS[side]):
                parts = [total[IG * ig + i, 0:USED, 38 * p:38 * p + 38] for i in range(IG)]
                parts.append(jnp.zeros((USED, LANES - 38 * IG), F32))
                tiles[side, d, u, USED * s:USED * (s + 1), :] = jnp.concatenate(parts, axis=1)
        for d in range(4):
            outs[d][...] = tiles[side, d]


def add_parts(info, own, got):
    outs = pl.pallas_call(
        add_kernel,
        out_shape=[jax.ShapeDtypeStruct((4, 2 * USED, LANES), F32)] * 8,
        in_specs=[SMEM, VM, VM],
        out_specs=[VM] * 8,
        scratch_shapes=[pltpu.VMEM(own.shape, F32), pltpu.VMEM((2, 4, 4, 2 * USED, LANES), F32)],
        compiler_params=PARAMS,
    )(info, own, got)
    return outs[:4], outs[4:]


def sum_kernel(*refs):
    ins, outs = refs[:4], refs[4:]
    for u in range(4):
        outs[u][...] = (ins[0][u] + ins[1][u]) + (ins[2][u] + ins[3][u])


def sum_parts(parts):
    rows = parts[0].shape[1]
    return pl.pallas_call(
        sum_kernel,
        out_shape=[jax.ShapeDtypeStruct((rows, LANES), F32)] * 4,
        in_specs=[VM] * 4,
        out_specs=[VM] * 4,
        compiler_params=PARAMS,
    )(*parts)


def dense_kernel(info, *refs):
    sides, outs, full = (refs[:4], refs[4:8]), refs[8:16], refs[16]
    me, z, r = info[0], info[1], info[2]
    ends = ends_of(info)
    first, number, _ = groups_of(ends, r)
    bp = lax.broadcasted_iota(I32, (BLK * CL, 1), 0)
    group, base = jnp.full_like(bp, -1), jnp.zeros_like(bp)
    for g in range(G):
        inside = (bp >= first[g]) & (bp < first[g] + number[g])
        group = jnp.where(inside, g, group)
        base = jnp.where(inside, first[g], base)
    for side, part in enumerate(sides):
        x = (part[0][...] + part[1][...]) + (part[2][...] + part[3][...])
        hi, mid = split(x)
        lo = ((x - hi.astype(F32)) - mid.astype(F32)).astype(BF16)
        window = lax.broadcasted_iota(I32, (BLK * CL, x.shape[0]), 1)
        for s, ig in enumerate(PARTS[side]):
            pick = (window == bp - base + USED * s).astype(F32).astype(BF16)
            y = jnp.dot(pick, hi, preferred_element_type=F32)
            y = y + jnp.dot(pick, mid, preferred_element_type=F32)
            y = y + jnp.dot(pick, lo, preferred_element_type=F32)
            y = jnp.where(group == lane_target(ends, info, ig, me), y, 0.0)
            for b in range(BLK):
                full[b, CL * ig:CL * (ig + 1), :] = y[CL * b:CL * (b + 1), :]
    for d in range(BLK):
        outs[d][...] = full[z ^ d]


def dense(info, a_parts, b_parts):
    return pl.pallas_call(
        dense_kernel,
        out_shape=[jax.ShapeDtypeStruct((NIG * CL, LANES), F32)] * BLK,
        in_specs=[SMEM] + [VM] * 8,
        out_specs=[VM] * BLK,
        scratch_shapes=[pltpu.VMEM((BLK, NIG * CL, LANES), F32)],
        compiler_params=PARAMS,
    )(info, *a_parts, *b_parts)


def final_kernel(*refs):
    ins, out = refs[:BLK], refs[BLK]
    for ig in range(NIG):
        parts = [ins[d][CL * ig:CL * (ig + 1), :] for d in range(BLK)]
        x = ((parts[0] + parts[1]) + (parts[2] + parts[3])) + ((parts[4] + parts[5]) + (parts[6] + parts[7]))
        y = x.T
        for i in range(IG):
            out[IG * ig + i, :, 0, :] = y[38 * i:38 * i + 38, :]


def final(parts):
    return pl.pallas_call(
        final_kernel,
        out_shape=jax.ShapeDtypeStruct((NI, CL, 1, CL), F32),
        in_specs=[VM] * BLK,
        out_specs=VM,
        compiler_params=PARAMS,
    )(*parts)


def exchange(parts, axis, step, size):
    got = [parts[0]]
    for d in range(1, len(parts)):
        got.append(lax.ppermute(parts[d], axis, [(p, p ^ (step * d)) for p in range(size)]))
    return got


def per_device(amplitudes, integrals, virt_sizes, i_irrep, j_irrep):
    p, z, r = lax.axis_index("pair"), lax.axis_index("blk"), lax.axis_index("rep")
    info = jnp.concatenate([jnp.stack([p, z, r]).astype(I32), virt_sizes, i_irrep, j_irrep])
    t = jnp.swapaxes(amplitudes, 2, 3)
    own, other = main(info, integrals, t)
    stage = add_parts(info, own, lax.ppermute(other, "rep", [(0, 1), (1, 0)]))
    stage = [exchange(stage[0], "pair", 1, PAIR), exchange(stage[1], "pair", 4, PAIR)]
    stage = [sum_parts(s) for s in stage]
    stage = [exchange(stage[0], "pair", 4, PAIR), exchange(stage[1], "pair", 1, PAIR)]
    parts = dense(info, *stage)
    return final(exchange(parts, "blk", 1, BLK))


def solution(mesh):
    return jax.shard_map(
        per_device,
        mesh=mesh,
        in_specs=(
            P(None, ("blk", "rep"), None, "pair"),
            P(("blk", "rep"), None, None, None),
            P(),
            P(),
            P(),
        ),
        out_specs=P(None, "pair", None, ("blk", "rep")),
        check_vma=False,
    )
```

```python
import functools

import jax
import jax.numpy as jnp
from jax import lax
from jax.experimental import pallas as pl
from jax.experimental.pallas import tpu as pltpu
from jax.sharding import PartitionSpec as P

NI, KL, CL, V, G = 12, 5, 38, 608, 8
PAIR, BLK = 16, 8
KP = 208
WIN = 80
SEG = 360
IG = 3
NIG = NI // IG
PARTS = ((0, 1), (2, 3))
LANES = 128
WIDE = 640
CUTS = (0, 192, 384, 560, 720)
NC = NI // 2
USED = 76
F32, BF16, I32 = jnp.float32, jnp.bfloat16, jnp.int32
SMEM = pl.BlockSpec(memory_space=pltpu.SMEM)
VM = pl.BlockSpec(memory_space=pltpu.VMEM)
HBM = pl.BlockSpec(memory_space=pltpu.HBM)
PARAMS = pltpu.CompilerParams(vmem_limit_bytes=16 * 1024 * 1024)
LARGE = pltpu.CompilerParams(vmem_limit_bytes=48 * 1024 * 1024)


def ends_of(info):
    ends, total = [], jnp.int32(0)
    for g in range(G):
        total = total + info[3 + g]
        ends.append(total)
    return ends


def below(x, r):
    full = (x * 863) >> 16
    return 38 * full + jnp.clip(x - 76 * full - 38 * r, 0, 38)


def groups_of(ends, r):
    first, number, offset = [], [], []
    last, row = jnp.int32(0), jnp.int32(0)
    for g in range(G):
        here = below(ends[g], r)
        first.append(last)
        number.append(here - last)
        offset.append(row)
        row = row + (((here - last) + 7) >> 3) * 8
        last = here
    return first, number, offset


def flip_of(info, i):
    return info[11 + i] ^ info[23]


def lane_target(ends, info, ig, p):
    lane = lax.broadcasted_iota(I32, (1, LANES), 1)
    second, third = lane >= 38, lane >= 76
    a = 38 * p + lane - jnp.where(third, 76, jnp.where(second, 38, 0))
    irrep = jnp.zeros((1, LANES), I32)
    for g in range(G):
        irrep = irrep + (a >= ends[g]).astype(I32)
    h = [flip_of(info, IG * ig + i) for i in range(IG)]
    h = jnp.where(third, h[2], jnp.where(second, h[1], h[0]))
    return irrep ^ h


def split(x):
    hi = x.astype(BF16)
    return hi, (x - hi.astype(F32)).astype(BF16)


def window_rows(info, r, wk, out_ref):
    ends = ends_of(info)
    hi, lo = split(wk[...])
    nt = (((1,), (1,)), ((), ()))
    for seg in range(2):
        rs = r ^ seg
        first, number, offset = groups_of(ends, rs)
        row = lax.broadcasted_iota(I32, (SEG, 1), 0)
        bp = jnp.full((SEG, 1), -1, I32)
        for g in range(G):
            inside = (row >= offset[g]) & (row < offset[g] + number[g])
            bp = jnp.where(inside, row - offset[g] + first[g], bp)
        b = jnp.where(bp < 0, -1, bp + 38 * ((bp * 1725) >> 16) + 38 * rs)
        pick = (lax.broadcasted_iota(I32, (SEG, V), 1) == b).astype(F32).astype(BF16)
        rows = slice(seg * SEG, (seg + 1) * SEG)
        wh = lax.dot_general(pick, hi, nt, preferred_element_type=F32).astype(BF16)
        wl = lax.dot_general(pick, lo, nt, preferred_element_type=F32).astype(BF16)
        out_ref[rows, 0:KP] = wh
        out_ref[rows, KP:2 * KP] = wh
        out_ref[rows, 2 * KP:3 * KP] = wl


def main_kernel(i0, info, w_in, t_hbm, own_ref, oth_ref, *refs):
    r = info[2]
    if i0 == 0:
        rows_ref, raw, wk, raw_sem = refs[:4]
        at = info[0] * CL
        raws = [pltpu.make_async_copy(w_in.at[k, pl.ds(at, CL)], raw.at[k], raw_sem.at[k]) for k in range(KL)]
    else:
        rows_ref, raws = w_in, []
    t_buf, x, t_all, d0, d1, in_sem = refs[-6:]
    loads = [pltpu.make_async_copy(t_hbm.at[i0 + n], t_buf.at[n], in_sem.at[n]) for n in range(NC)]
    for c in raws + loads:
        c.start()
    x[...] = jnp.zeros_like(x)
    for d in (d0, d1):
        d[2 * SEG:, :] = jnp.zeros((WIN, 2 * LANES), F32)
    if i0 == 0:
        wk[...] = jnp.zeros_like(wk)
        for c in raws:
            c.wait()
        for k in range(KL):
            wk[40 * k:40 * k + CL, :] = raw[k, :, 0, :]
        window_rows(info, r, wk, rows_ref)
    ends = ends_of(info)
    offsets = [groups_of(ends, r ^ seg)[2] for seg in range(2)]
    lane = lax.broadcasted_iota(I32, (1, WIDE), 1)
    irrep = jnp.zeros((1, WIDE), I32)
    for g in range(G):
        irrep = irrep + (lane >= ends[g]).astype(I32)

    def prepare(n):
        loads[n].wait()
        slot, odd = (n // 2) % 2, n % 2
        for k in range(KL):
            x[n % 2, 40 * k:40 * k + CL, 0:V] = t_buf[n, k]
        for c in range(5):
            tile, half = (2, odd) if c == 4 else (3 * odd + c // 2, c % 2)
            lanes = slice(half * LANES, (half + 1) * LANES)
            hi, lo = split(x[n % 2, :, c * LANES:(c + 1) * LANES])
            t_all[slot, tile, 0:KP, lanes] = hi
            t_all[slot, tile, KP:2 * KP, lanes] = lo
            t_all[slot, tile, 2 * KP:3 * KP, lanes] = hi

    def select(u, half, seg):
        pair, tile = units[u]
        d = (d0, d1)[u % 2]
        if tile == 2:
            n, c = 2 * pair + half, 4
        else:
            n, c = 2 * pair + tile // 3, 2 * (tile % 3) + half
        target = irrep[:, c * LANES:(c + 1) * LANES] ^ flip_of(info, i0 + n)
        acc = None
        for g in range(G):
            start = pl.multiple_of(seg * SEG + offsets[seg][g], 8)
            part = d[pl.ds(start, WIN), half * LANES:(half + 1) * LANES]
            acc = part if g == 0 else jnp.where(target == g, part, acc)
        (own_ref, oth_ref)[seg][n, :, c * LANES:(c + 1) * LANES] = acc

    units = [divmod(u, 5) for u in range(5 * NC // 2)]
    prepare(0)
    prepare(1)
    pieces = [(half, seg) for half in range(2) for seg in range(2)]
    for u in range(len(units)):
        pair, tile = units[u]
        for m, (half, seg) in enumerate(pieces):
            rows = slice(CUTS[m], CUTS[m + 1])
            (d0, d1)[u % 2][rows, :] = jnp.dot(rows_ref[rows, :], t_all[pair % 2, tile], preferred_element_type=F32)
            if u:
                select(u - 1, half, seg)
        if tile in (0, 2) and 2 * pair + 2 < NC:
            prepare(2 * pair + 2 + tile // 2)
    for half, seg in pieces:
        select(len(units) - 1, half, seg)


def main(i0, info, w, t):
    packed = jax.ShapeDtypeStruct((NC, WIN, WIDE), F32)
    rows = jax.ShapeDtypeStruct((2 * SEG, 3 * KP), BF16)
    hbm = pl.BlockSpec(memory_space=pl.ANY)
    extra = [pltpu.VMEM((KL, CL, 1, V), F32), pltpu.VMEM((KP, V), F32), pltpu.SemaphoreType.DMA((KL,))]
    return pl.pallas_call(
        functools.partial(main_kernel, i0),
        out_shape=(packed, packed) if i0 else (packed, packed, rows),
        in_specs=[SMEM, VM if i0 else hbm, hbm],
        out_specs=(VM, VM) if i0 else (VM, VM, VM),
        scratch_shapes=([] if i0 else extra) + [
            pltpu.VMEM((NC, KL, CL, V), F32),
            pltpu.VMEM((2, KP, WIDE), F32),
            pltpu.VMEM((2, 5, 3 * KP, 2 * LANES), BF16),
            pltpu.VMEM((2 * SEG + WIN, 2 * LANES), F32),
            pltpu.VMEM((2 * SEG + WIN, 2 * LANES), F32),
            pltpu.SemaphoreType.DMA((NC,)),
        ],
        compiler_params=LARGE,
        cost_estimate=pl.CostEstimate(flops=6000000000, bytes_accessed=6000000, transcendentals=0),
    )(info, w, t)


def add_kernel(side, info, own_ref, got_ref, *refs):
    outs, total, tiles, sem = refs[:4], refs[4], refs[5], refs[6]
    me = info[0]
    total[...] = own_ref[...] + got_ref[...]
    for p in range(PAIR):
        rel = p ^ me
        low, high = rel & 3, rel >> 2
        d, u = (high, low) if side else (low, high)
        for s in range(2):
            parts = [total[IG * s + i, 0:USED, 38 * p:38 * p + 38] for i in range(IG)]
            parts.append(jnp.zeros((USED, LANES - 38 * IG), F32))
            tiles[d, u, USED * s:USED * (s + 1), :] = jnp.concatenate(parts, axis=1)
    copies = [pltpu.make_async_copy(tiles.at[d], outs[d], sem.at[d]) for d in range(4)]
    for c in copies:
        c.start()
    for c in copies:
        c.wait()


def add_parts(side, info, own, got):
    return pl.pallas_call(
        functools.partial(add_kernel, side),
        out_shape=[jax.ShapeDtypeStruct((4, 2 * USED, LANES), F32)] * 4,
        in_specs=[SMEM, VM, VM],
        out_specs=[HBM] * 4,
        scratch_shapes=[pltpu.VMEM(own.shape, F32), pltpu.VMEM((4, 4, 2 * USED, LANES), F32),
                        pltpu.SemaphoreType.DMA((4,))],
        compiler_params=PARAMS,
        cost_estimate=pl.CostEstimate(flops=1000000, bytes_accessed=4000000, transcendentals=0),
    )(info, own, got)


def sum_kernel(*refs):
    ins, outs, buf, sem = refs[:4], refs[4:8], refs[8], refs[9]
    copies = [pltpu.make_async_copy(ins[d], buf.at[d], sem.at[d]) for d in range(4)]
    for c in copies:
        c.start()
    for c in copies:
        c.wait()
    for u in range(4):
        outs[u][...] = (buf[0, u] + buf[1, u]) + (buf[2, u] + buf[3, u])


def sum_parts(parts):
    return pl.pallas_call(
        sum_kernel,
        out_shape=[jax.ShapeDtypeStruct((2 * USED, LANES), F32)] * 4,
        in_specs=[HBM] * 4,
        out_specs=[VM] * 4,
        scratch_shapes=[pltpu.VMEM((4, 4, 2 * USED, LANES), F32), pltpu.SemaphoreType.DMA((4,))],
        compiler_params=PARAMS,
    )(*parts)


def dense_kernel(info, *refs):
    sides, outs, full = (refs[:4], refs[4:8]), refs[8:16], refs[16]
    me, z, r = info[0], info[1], info[2]
    ends = ends_of(info)
    first, number, _ = groups_of(ends, r)
    bp = lax.broadcasted_iota(I32, (BLK * CL, 1), 0)
    group, base = jnp.full_like(bp, -1), jnp.zeros_like(bp)
    for g in range(G):
        inside = (bp >= first[g]) & (bp < first[g] + number[g])
        group = jnp.where(inside, g, group)
        base = jnp.where(inside, first[g], base)
    for side, part in enumerate(sides):
        x = (part[0][...] + part[1][...]) + (part[2][...] + part[3][...])
        hi, mid = split(x)
        lo = ((x - hi.astype(F32)) - mid.astype(F32)).astype(BF16)
        window = lax.broadcasted_iota(I32, (BLK * CL, x.shape[0]), 1)
        for s, ig in enumerate(PARTS[side]):
            pick = (window == bp - base + USED * s).astype(F32).astype(BF16)
            y = jnp.dot(pick, hi, preferred_element_type=F32)
            y = y + jnp.dot(pick, mid, preferred_element_type=F32)
            y = y + jnp.dot(pick, lo, preferred_element_type=F32)
            y = jnp.where(group == lane_target(ends, info, ig, me), y, 0.0)
            for b in range(BLK):
                full[b, CL * ig:CL * (ig + 1), :] = y[CL * b:CL * (b + 1), :]
    for d in range(BLK):
        outs[d][...] = full[z ^ d]


def dense(info, a_parts, b_parts):
    return pl.pallas_call(
        dense_kernel,
        out_shape=[jax.ShapeDtypeStruct((NIG * CL, LANES), F32)] * BLK,
        in_specs=[SMEM] + [VM] * 8,
        out_specs=[VM] * BLK,
        scratch_shapes=[pltpu.VMEM((BLK, NIG * CL, LANES), F32)],
        compiler_params=PARAMS,
    )(info, *a_parts, *b_parts)


def final_kernel(*refs):
    ins, out = refs[:BLK], refs[BLK]
    for ig in range(NIG):
        parts = [ins[d][CL * ig:CL * (ig + 1), :] for d in range(BLK)]
        x = ((parts[0] + parts[1]) + (parts[2] + parts[3])) + ((parts[4] + parts[5]) + (parts[6] + parts[7]))
        y = x.T
        for i in range(IG):
            out[IG * ig + i, :, 0, :] = y[38 * i:38 * i + 38, :]


def final(parts):
    return pl.pallas_call(
        final_kernel,
        out_shape=jax.ShapeDtypeStruct((NI, CL, 1, CL), F32),
        in_specs=[VM] * BLK,
        out_specs=VM,
        compiler_params=PARAMS,
    )(*parts)


def exchange(parts, axis, step, size):
    got = [parts[0]]
    for d in range(1, len(parts)):
        got.append(lax.ppermute(parts[d], axis, [(p, p ^ (step * d)) for p in range(size)]))
    return got


def per_device(amplitudes, integrals, virt_sizes, i_irrep, j_irrep):
    p, z, r = lax.axis_index("pair"), lax.axis_index("blk"), lax.axis_index("rep")
    info = jnp.concatenate([jnp.stack([p, z, r]).astype(I32), virt_sizes, i_irrep, j_irrep])
    t = jnp.swapaxes(amplitudes, 2, 3)
    swap = [(0, 1), (1, 0)]
    own, other, rows = main(0, info, integrals, t)
    packed = [(own, other), main(NC, info, rows, t)]
    stage = [add_parts(side, info, own, lax.ppermute(other, "rep", swap)) for side, (own, other) in enumerate(packed)]
    stage = [exchange(stage[0], "pair", 1, PAIR), exchange(stage[1], "pair", 4, PAIR)]
    stage = [sum_parts(s) for s in stage]
    stage = [exchange(stage[0], "pair", 4, PAIR), exchange(stage[1], "pair", 1, PAIR)]
    parts = dense(info, *stage)
    return final(exchange(parts, "blk", 1, BLK))


def solution(mesh):
    return jax.shard_map(
        per_device,
        mesh=mesh,
        in_specs=(
            P(None, ("blk", "rep"), None, "pair"),
            P(("blk", "rep"), None, None, None),
            P(),
            P(),
            P(),
        ),
        out_specs=P(None, "pair", None, ("blk", "rep")),
        check_vma=False,
    )
```

```python
import functools

import jax
import jax.numpy as jnp
from jax import lax
from jax.experimental import pallas as pl
from jax.experimental.pallas import tpu as pltpu
from jax.sharding import PartitionSpec as P

NI, KL, CL, V, G = 12, 5, 38, 608, 8
PAIR, BLK = 16, 8
KP = 208
WIN = 80
SEG = 360
IG = 3
NIG = NI // IG
PARTS = ((0, 1), (2, 3))
LANES = 128
WIDE = 640
CUTS = (0, 192, 384, 560, 720)
NC = NI // 2
FAR = (0, 3, 5, 7)
USED = 76
F32, BF16, I32 = jnp.float32, jnp.bfloat16, jnp.int32
SMEM = pl.BlockSpec(memory_space=pltpu.SMEM)
VM = pl.BlockSpec(memory_space=pltpu.VMEM)
HBM = pl.BlockSpec(memory_space=pltpu.HBM)
PARAMS = pltpu.CompilerParams(vmem_limit_bytes=16 * 1024 * 1024)
LARGE = pltpu.CompilerParams(vmem_limit_bytes=48 * 1024 * 1024)


def ends_of(info):
    ends, total = [], jnp.int32(0)
    for g in range(G):
        total = total + info[3 + g]
        ends.append(total)
    return ends


def below(x, r):
    full = (x * 863) >> 16
    return 38 * full + jnp.clip(x - 76 * full - 38 * r, 0, 38)


def groups_of(ends, r):
    first, number, offset = [], [], []
    last, row = jnp.int32(0), jnp.int32(0)
    for g in range(G):
        here = below(ends[g], r)
        first.append(last)
        number.append(here - last)
        offset.append(row)
        row = row + (((here - last) + 7) >> 3) * 8
        last = here
    return first, number, offset


def flip_of(info, i):
    return info[11 + i] ^ info[23]


def lane_target(ends, info, ig, p):
    lane = lax.broadcasted_iota(I32, (1, LANES), 1)
    second, third = lane >= 38, lane >= 76
    a = 38 * p + lane - jnp.where(third, 76, jnp.where(second, 38, 0))
    irrep = jnp.zeros((1, LANES), I32)
    for g in range(G):
        irrep = irrep + (a >= ends[g]).astype(I32)
    h = [flip_of(info, IG * ig + i) for i in range(IG)]
    h = jnp.where(third, h[2], jnp.where(second, h[1], h[0]))
    return irrep ^ h


def split(x):
    hi = x.astype(BF16)
    return hi, (x - hi.astype(F32)).astype(BF16)


def window_rows(info, r, wk, out_ref):
    ends = ends_of(info)
    hi, lo = split(wk[...])
    nt = (((1,), (1,)), ((), ()))
    for seg in range(2):
        rs = r ^ seg
        first, number, offset = groups_of(ends, rs)
        row = lax.broadcasted_iota(I32, (SEG, 1), 0)
        bp = jnp.full((SEG, 1), -1, I32)
        for g in range(G):
            inside = (row >= offset[g]) & (row < offset[g] + number[g])
            bp = jnp.where(inside, row - offset[g] + first[g], bp)
        b = jnp.where(bp < 0, -1, bp + 38 * ((bp * 1725) >> 16) + 38 * rs)
        pick = (lax.broadcasted_iota(I32, (SEG, V), 1) == b).astype(F32).astype(BF16)
        rows = slice(seg * SEG, (seg + 1) * SEG)
        wh = lax.dot_general(pick, hi, nt, preferred_element_type=F32).astype(BF16)
        wl = lax.dot_general(pick, lo, nt, preferred_element_type=F32).astype(BF16)
        out_ref[rows, 0:KP] = wh
        out_ref[rows, KP:2 * KP] = wh
        out_ref[rows, 2 * KP:3 * KP] = wl


def main_kernel(i0, info, w_in, t_hbm, own_ref, oth_ref, *refs):
    r = info[2]
    if i0 == 0:
        rows_ref, raw, wk, raw_sem = refs[:4]
        at = info[0] * CL
        raws = [pltpu.make_async_copy(w_in.at[k, pl.ds(at, CL)], raw.at[k], raw_sem.at[k]) for k in range(KL)]
    else:
        rows_ref, raws = w_in, []
    t_buf, x, t_all, d0, d1, in_sem = refs[-6:]
    loads = [pltpu.make_async_copy(t_hbm.at[i0 + n], t_buf.at[n], in_sem.at[n]) for n in range(NC)]
    for c in raws + loads:
        c.start()
    x[...] = jnp.zeros_like(x)
    for d in (d0, d1):
        d[2 * SEG:, :] = jnp.zeros((WIN, 2 * LANES), F32)
    if i0 == 0:
        wk[...] = jnp.zeros_like(wk)
        for c in raws:
            c.wait()
        for k in range(KL):
            wk[40 * k:40 * k + CL, :] = raw[k, :, 0, :]
        window_rows(info, r, wk, rows_ref)
    ends = ends_of(info)
    offsets = [groups_of(ends, r ^ seg)[2] for seg in range(2)]
    lane = lax.broadcasted_iota(I32, (1, WIDE), 1)
    irrep = jnp.zeros((1, WIDE), I32)
    for g in range(G):
        irrep = irrep + (lane >= ends[g]).astype(I32)

    def prepare(n):
        loads[n].wait()
        slot, odd = (n // 2) % 2, n % 2
        for k in range(KL):
            x[n % 2, 40 * k:40 * k + CL, 0:V] = t_buf[n, k]
        for c in range(5):
            tile, half = (2, odd) if c == 4 else (3 * odd + c // 2, c % 2)
            lanes = slice(half * LANES, (half + 1) * LANES)
            hi, lo = split(x[n % 2, :, c * LANES:(c + 1) * LANES])
            t_all[slot, tile, 0:KP, lanes] = hi
            t_all[slot, tile, KP:2 * KP, lanes] = lo
            t_all[slot, tile, 2 * KP:3 * KP, lanes] = hi

    def select(u, half, seg):
        pair, tile = units[u]
        d = (d0, d1)[u % 2]
        if tile == 2:
            n, c = 2 * pair + half, 4
        else:
            n, c = 2 * pair + tile // 3, 2 * (tile % 3) + half
        target = irrep[:, c * LANES:(c + 1) * LANES] ^ flip_of(info, i0 + n)
        acc = None
        for g in range(G):
            start = pl.multiple_of(seg * SEG + offsets[seg][g], 8)
            part = d[pl.ds(start, WIN), half * LANES:(half + 1) * LANES]
            acc = part if g == 0 else jnp.where(target == g, part, acc)
        (own_ref, oth_ref)[seg][n, :, c * LANES:(c + 1) * LANES] = acc

    units = [divmod(u, 5) for u in range(5 * NC // 2)]
    prepare(0)
    prepare(1)
    pieces = [(half, seg) for half in range(2) for seg in range(2)]
    for u in range(len(units)):
        pair, tile = units[u]
        for m, (half, seg) in enumerate(pieces):
            rows = slice(CUTS[m], CUTS[m + 1])
            (d0, d1)[u % 2][rows, :] = jnp.dot(rows_ref[rows, :], t_all[pair % 2, tile], preferred_element_type=F32)
            if u:
                select(u - 1, half, seg)
        if tile in (0, 2) and 2 * pair + 2 < NC:
            prepare(2 * pair + 2 + tile // 2)
    for half, seg in pieces:
        select(len(units) - 1, half, seg)


def main(i0, info, w, t):
    packed = jax.ShapeDtypeStruct((NC, WIN, WIDE), F32)
    rows = jax.ShapeDtypeStruct((2 * SEG, 3 * KP), BF16)
    hbm = pl.BlockSpec(memory_space=pl.ANY)
    extra = [pltpu.VMEM((KL, CL, 1, V), F32), pltpu.VMEM((KP, V), F32), pltpu.SemaphoreType.DMA((KL,))]
    return pl.pallas_call(
        functools.partial(main_kernel, i0),
        out_shape=(packed, packed) if i0 else (packed, packed, rows),
        in_specs=[SMEM, VM if i0 else hbm, hbm],
        out_specs=(VM, VM) if i0 else (VM, VM, VM),
        scratch_shapes=([] if i0 else extra) + [
            pltpu.VMEM((NC, KL, CL, V), F32),
            pltpu.VMEM((2, KP, WIDE), F32),
            pltpu.VMEM((2, 5, 3 * KP, 2 * LANES), BF16),
            pltpu.VMEM((2 * SEG + WIN, 2 * LANES), F32),
            pltpu.VMEM((2 * SEG + WIN, 2 * LANES), F32),
            pltpu.SemaphoreType.DMA((NC,)),
        ],
        compiler_params=LARGE,
        cost_estimate=pl.CostEstimate(flops=6000000000, bytes_accessed=6000000, transcendentals=0),
    )(info, w, t)


def add_kernel(side, info, own_ref, got_ref, *refs):
    outs, total, tiles, sem = refs[:4], refs[4], refs[5], refs[6]
    me = info[0]
    total[...] = own_ref[...] + got_ref[...]
    for p in range(PAIR):
        rel = p ^ me
        low, high = rel & 3, rel >> 2
        d, u = (high, low) if side else (low, high)
        for s in range(2):
            parts = [total[IG * s + i, 0:USED, 38 * p:38 * p + 38] for i in range(IG)]
            parts.append(jnp.zeros((USED, LANES - 38 * IG), F32))
            tiles[d, u, USED * s:USED * (s + 1), :] = jnp.concatenate(parts, axis=1)
    copies = [pltpu.make_async_copy(tiles.at[d], outs[d], sem.at[d]) for d in range(4)]
    for c in copies:
        c.start()
    for c in copies:
        c.wait()


def add_parts(side, info, own, got):
    return pl.pallas_call(
        functools.partial(add_kernel, side),
        out_shape=[jax.ShapeDtypeStruct((4, 2 * USED, LANES), F32)] * 4,
        in_specs=[SMEM, VM, VM],
        out_specs=[HBM] * 4,
        scratch_shapes=[pltpu.VMEM(own.shape, F32), pltpu.VMEM((4, 4, 2 * USED, LANES), F32),
                        pltpu.SemaphoreType.DMA((4,))],
        compiler_params=PARAMS,
        cost_estimate=pl.CostEstimate(flops=1000000, bytes_accessed=4000000, transcendentals=0),
    )(info, own, got)


def sum_kernel(*refs):
    ins, outs, buf, sem = refs[:8], refs[8:16], refs[16], refs[17]
    copies = [pltpu.make_async_copy(ins[d], buf.at[d], sem.at[d]) for d in range(8)]
    for c in copies:
        c.start()
    for side in (0, 4):
        for d in range(4):
            copies[side + d].wait()
        for u in range(4):
            outs[side + u][...] = (buf[side, u] + buf[side + 1, u]) + (buf[side + 2, u] + buf[side + 3, u])


def sum_parts(a_parts, b_parts):
    outs = pl.pallas_call(
        sum_kernel,
        out_shape=[jax.ShapeDtypeStruct((2 * USED, LANES), F32)] * 8,
        in_specs=[HBM] * 8,
        out_specs=[VM] * 8,
        scratch_shapes=[pltpu.VMEM((8, 4, 2 * USED, LANES), F32), pltpu.SemaphoreType.DMA((8,))],
        compiler_params=PARAMS,
    )(*a_parts, *b_parts)
    return outs[:4], outs[4:]


def join_kernel(*refs):
    out = refs[8]
    for side in range(2):
        parts = [ref[...] for ref in refs[4 * side:4 * side + 4]]
        out[side] = (parts[0] + parts[1]) + (parts[2] + parts[3])


def join(a_parts, b_parts):
    return pl.pallas_call(
        join_kernel,
        out_shape=jax.ShapeDtypeStruct((2, 2 * USED, LANES), F32),
        in_specs=[VM] * 8,
        out_specs=VM,
        compiler_params=PARAMS,
    )(*a_parts, *b_parts)


def dense_kernel(info, *refs):
    mine, got, outs, full = refs[0], refs[1], refs[2:-1], refs[-1]
    me, z, r = info[0], info[1], info[2]
    ends = ends_of(info)
    first, number, _ = groups_of(ends, r)
    bp = lax.broadcasted_iota(I32, (BLK * CL, 1), 0)
    group, base = jnp.full_like(bp, -1), jnp.zeros_like(bp)
    for g in range(G):
        inside = (bp >= first[g]) & (bp < first[g] + number[g])
        group = jnp.where(inside, g, group)
        base = jnp.where(inside, first[g], base)
    for side in range(2):
        x = mine[side] + got[side]
        hi, mid = split(x)
        lo = ((x - hi.astype(F32)) - mid.astype(F32)).astype(BF16)
        window = lax.broadcasted_iota(I32, (BLK * CL, x.shape[0]), 1)
        for s, ig in enumerate(PARTS[side]):
            pick = (window == bp - base + USED * s).astype(F32).astype(BF16)
            y = jnp.dot(pick, hi, preferred_element_type=F32)
            y = y + jnp.dot(pick, mid, preferred_element_type=F32)
            y = y + jnp.dot(pick, lo, preferred_element_type=F32)
            y = jnp.where(group == lane_target(ends, info, ig, me), y, 0.0)
            for b in range(BLK):
                full[b, CL * ig:CL * (ig + 1), :] = y[CL * b:CL * (b + 1), :]
    for n, d in enumerate(FAR):
        outs[n][...] = full[z ^ d]


def dense(info, mine, got):
    return pl.pallas_call(
        dense_kernel,
        out_shape=[jax.ShapeDtypeStruct((NIG * CL, LANES), F32)] * len(FAR),
        in_specs=[SMEM, VM, VM],
        out_specs=[VM] * len(FAR),
        scratch_shapes=[pltpu.VMEM((BLK, NIG * CL, LANES), F32)],
        compiler_params=PARAMS,
    )(info, mine, got)


def final_kernel(*refs):
    ins, out = refs[:-1], refs[-1]
    for ig in range(NIG):
        parts = [ref[CL * ig:CL * (ig + 1), :] for ref in ins]
        x = (parts[0] + parts[1]) + (parts[2] + parts[3])
        y = x.T
        for i in range(IG):
            out[IG * ig + i, :, 0, :] = y[38 * i:38 * i + 38, :]


def final(parts):
    return pl.pallas_call(
        final_kernel,
        out_shape=jax.ShapeDtypeStruct((NI, CL, 1, CL), F32),
        in_specs=[VM] * len(FAR),
        out_specs=VM,
        compiler_params=PARAMS,
    )(*parts)


def swap(x, axis, step, size):
    return lax.ppermute(x, axis, [(p, p ^ step) for p in range(size)])


def exchange(parts, step, order):
    return [parts[0]] + [swap(parts[d], "pair", step * d, PAIR) for d in order]


def per_device(amplitudes, integrals, virt_sizes, i_irrep, j_irrep):
    p, z, r = lax.axis_index("pair"), lax.axis_index("blk"), lax.axis_index("rep")
    info = jnp.concatenate([jnp.stack([p, z, r]).astype(I32), virt_sizes, i_irrep, j_irrep])
    t = jnp.swapaxes(amplitudes, 2, 3)
    own, other, rows = main(0, info, integrals, t)
    packed = [(own, other), main(NC, info, rows, t)]
    a, b = [add_parts(side, info, own, swap(other, "rep", 1, 2)) for side, (own, other) in enumerate(packed)]
    a, b = lax.optimization_barrier((a, b))
    a, b = exchange(a, 1, (2, 3, 1)), exchange(b, 4, (2, 3, 1))
    a, b = sum_parts(*lax.optimization_barrier((a, b)))
    x = join(exchange(a, 4, (2, 1, 3)), exchange(b, 1, (2, 1, 3)))
    parts = dense(info, x, swap(x, "blk", 1, BLK))
    return final([parts[0]] + [swap(parts[n], "blk", FAR[n], BLK) for n in range(1, len(FAR))])


def solution(mesh):
    return jax.shard_map(
        per_device,
        mesh=mesh,
        in_specs=(
            P(None, ("blk", "rep"), None, "pair"),
            P(("blk", "rep"), None, None, None),
            P(),
            P(),
            P(),
        ),
        out_specs=P(None, "pair", None, ("blk", "rep")),
        check_vma=False,
    )
```

```python
import functools

import jax
import jax.numpy as jnp
from jax import lax
from jax.experimental import pallas as pl
from jax.experimental.pallas import tpu as pltpu
from jax.sharding import PartitionSpec as P

NI, KL, CL, V, G = 12, 5, 38, 608, 8
PAIR, BLK = 16, 8
KP = 208
WIN = 152
SEG = 672
IG = 3
NC = NI // 2
LANES = 128
CUTS = (0, 336, 672)
WIDE = 640
FAR = (0, 3, 5, 7)
F32, BF16, I32 = jnp.float32, jnp.bfloat16, jnp.int32
SMEM = pl.BlockSpec(memory_space=pltpu.SMEM)
VM = pl.BlockSpec(memory_space=pltpu.VMEM)
HBM = pl.BlockSpec(memory_space=pltpu.HBM)
PARAMS = pltpu.CompilerParams(vmem_limit_bytes=16 * 1024 * 1024)
LARGE = pltpu.CompilerParams(vmem_limit_bytes=48 * 1024 * 1024)


def ends_of(info):
    ends, total = [], jnp.int32(0)
    for g in range(G):
        total = total + info[3 + g]
        ends.append(total)
    return ends


def groups_of(ends):
    first, number, offset = [], [], []
    last, row = jnp.int32(0), jnp.int32(0)
    for g in range(G):
        first.append(last)
        number.append(ends[g] - last)
        offset.append(row)
        row = row + ((ends[g] - last + 7) >> 3) * 8
        last = ends[g]
    return first, number, offset


def flip_of(info, i):
    return info[11 + i] ^ info[23]


def lane_target(ends, info, ig, p):
    lane = lax.broadcasted_iota(I32, (1, LANES), 1)
    second, third = lane >= 38, lane >= 76
    a = 38 * p + lane - jnp.where(third, 76, jnp.where(second, 38, 0))
    irrep = jnp.zeros((1, LANES), I32)
    for g in range(G):
        irrep = irrep + (a >= ends[g]).astype(I32)
    h = [flip_of(info, IG * ig + i) for i in range(IG)]
    h = jnp.where(third, h[2], jnp.where(second, h[1], h[0]))
    return irrep ^ h


def split(x):
    hi = x.astype(BF16)
    return hi, (x - hi.astype(F32)).astype(BF16)


def window_rows(info, wk, out_ref):
    first, number, offset = groups_of(ends_of(info))
    hi, lo = split(wk[...])
    nt = (((1,), (1,)), ((), ()))
    row = lax.broadcasted_iota(I32, (SEG, 1), 0)
    b = jnp.full((SEG, 1), -1, I32)
    for g in range(G):
        inside = (row >= offset[g]) & (row < offset[g] + number[g])
        b = jnp.where(inside, row - offset[g] + first[g], b)
    pick = (lax.broadcasted_iota(I32, (SEG, V), 1) == b).astype(F32).astype(BF16)
    wh = lax.dot_general(pick, hi, nt, preferred_element_type=F32).astype(BF16)
    wl = lax.dot_general(pick, lo, nt, preferred_element_type=F32).astype(BF16)
    out_ref[:, 0:KP] = wh
    out_ref[:, KP:2 * KP] = wh
    out_ref[:, 2 * KP:3 * KP] = wl


def main_kernel(own, info, w_in, t_hbm, out_ref, *refs):
    i0 = NC * (info[2] if own else 1 - info[2])
    if not own:
        rows_ref, raw, wk, raw_sem = refs[:4]
        at = info[0] * CL
        raws = [pltpu.make_async_copy(w_in.at[k, pl.ds(at, CL)], raw.at[k], raw_sem.at[k]) for k in range(KL)]
    else:
        rows_ref, raws = w_in, []
    t_buf, x, t_all, d0, d1, in_sem = refs[-6:]
    loads = [pltpu.make_async_copy(t_hbm.at[i0 + n], t_buf.at[n], in_sem.at[n]) for n in range(NC)]
    for c in raws + loads:
        c.start()
    x[...] = jnp.zeros_like(x)
    for d in (d0, d1):
        d[SEG:, :] = jnp.zeros((WIN, 2 * LANES), F32)
    if not own:
        wk[...] = jnp.zeros_like(wk)
        for c in raws:
            c.wait()
        for k in range(KL):
            wk[40 * k:40 * k + CL, :] = raw[k, :, 0, :]
        window_rows(info, wk, rows_ref)
    ends = ends_of(info)
    offsets = groups_of(ends)[2]
    lane = lax.broadcasted_iota(I32, (1, WIDE), 1)
    irrep = jnp.zeros((1, WIDE), I32)
    for g in range(G):
        irrep = irrep + (lane >= ends[g]).astype(I32)

    def prepare(n):
        loads[n].wait()
        slot, odd = (n // 2) % 2, n % 2
        for k in range(KL):
            x[n % 2, 40 * k:40 * k + CL, 0:V] = t_buf[n, k]
        for c in range(5):
            tile, half = (2, odd) if c == 4 else (3 * odd + c // 2, c % 2)
            lanes = slice(half * LANES, (half + 1) * LANES)
            hi, lo = split(x[n % 2, :, c * LANES:(c + 1) * LANES])
            t_all[slot, tile, 0:KP, lanes] = hi
            t_all[slot, tile, KP:2 * KP, lanes] = lo
            t_all[slot, tile, 2 * KP:3 * KP, lanes] = hi

    def select(u, half):
        pair, tile = units[u]
        d = (d0, d1)[u % 2]
        if tile == 2:
            n, c = 2 * pair + half, 4
        else:
            n, c = 2 * pair + tile // 3, 2 * (tile % 3) + half
        target = irrep[:, c * LANES:(c + 1) * LANES] ^ flip_of(info, i0 + n)
        acc = None
        for g in range(G):
            start = pl.multiple_of(offsets[g], 8)
            part = d[pl.ds(start, WIN), half * LANES:(half + 1) * LANES]
            acc = part if g == 0 else jnp.where(target == g, part, acc)
        out_ref[n, :, c * LANES:(c + 1) * LANES] = acc

    units = [divmod(u, 5) for u in range(5 * NC // 2)]
    prepare(0)
    prepare(1)
    for u in range(len(units)):
        pair, tile = units[u]
        for half in range(2):
            rows = slice(CUTS[half], CUTS[half + 1])
            (d0, d1)[u % 2][rows, :] = jnp.dot(rows_ref[rows, :], t_all[pair % 2, tile], preferred_element_type=F32)
            if u:
                select(u - 1, half)
        if tile in (0, 2) and 2 * pair + 2 < NC:
            prepare(2 * pair + 2 + tile // 2)
    for half in range(2):
        select(len(units) - 1, half)


def main(own, info, w, t):
    packed = jax.ShapeDtypeStruct((NC, WIN, WIDE), F32)
    rows = jax.ShapeDtypeStruct((SEG, 3 * KP), BF16)
    hbm = pl.BlockSpec(memory_space=pl.ANY)
    extra = [pltpu.VMEM((KL, CL, 1, V), F32), pltpu.VMEM((KP, V), F32), pltpu.SemaphoreType.DMA((KL,))]
    return pl.pallas_call(
        functools.partial(main_kernel, own),
        out_shape=(packed,) if own else (packed, rows),
        in_specs=[SMEM, VM if own else hbm, hbm],
        out_specs=(VM,) if own else (VM, VM),
        scratch_shapes=([] if own else extra) + [
            pltpu.VMEM((NC, KL, CL, V), F32),
            pltpu.VMEM((2, KP, WIDE), F32),
            pltpu.VMEM((2, 5, 3 * KP, 2 * LANES), BF16),
            pltpu.VMEM((SEG + WIN, 2 * LANES), F32),
            pltpu.VMEM((SEG + WIN, 2 * LANES), F32),
            pltpu.SemaphoreType.DMA((NC,)),
        ],
        compiler_params=LARGE,
        cost_estimate=pl.CostEstimate(flops=6000000000, bytes_accessed=6000000, transcendentals=0),
    )(info, w, t)


def add_kernel(info, own_ref, got_ref, *refs):
    outs, total, tiles, sem = refs[:4], refs[4], refs[5], refs[6]
    me, r = info[0], info[2]
    total[...] = own_ref[...] + got_ref[...]
    for p in range(PAIR):
        rel = p ^ me
        low, high = rel & 3, rel >> 2
        d, u = jnp.where(r == 0, low, high), jnp.where(r == 0, high, low)
        for s in range(2):
            parts = [total[IG * s + i, :, 38 * p:38 * p + 38] for i in range(IG)]
            parts.append(jnp.zeros((WIN, LANES - 38 * IG), F32))
            tiles[d, u, WIN * s:WIN * (s + 1), :] = jnp.concatenate(parts, axis=1)
    copies = [pltpu.make_async_copy(tiles.at[d], outs[d], sem.at[d]) for d in range(4)]
    for c in copies:
        c.start()
    for c in copies:
        c.wait()


def add_parts(info, own, got):
    return pl.pallas_call(
        add_kernel,
        out_shape=[jax.ShapeDtypeStruct((4, 2 * WIN, LANES), F32)] * 4,
        in_specs=[SMEM, VM, VM],
        out_specs=[HBM] * 4,
        scratch_shapes=[pltpu.VMEM(own.shape, F32), pltpu.VMEM((4, 4, 2 * WIN, LANES), F32),
                        pltpu.SemaphoreType.DMA((4,))],
        compiler_params=PARAMS,
        cost_estimate=pl.CostEstimate(flops=1000000, bytes_accessed=4000000, transcendentals=0),
    )(info, own, got)


def sum_kernel(*refs):
    ins, outs, buf, sem = refs[:4], refs[4:8], refs[8], refs[9]
    copies = [pltpu.make_async_copy(ins[d], buf.at[d], sem.at[d]) for d in range(4)]
    for c in copies:
        c.start()
    for c in copies:
        c.wait()
    for u in range(4):
        outs[u][...] = (buf[0, u] + buf[1, u]) + (buf[2, u] + buf[3, u])


def sum_parts(parts):
    return pl.pallas_call(
        sum_kernel,
        out_shape=[jax.ShapeDtypeStruct((2 * WIN, LANES), F32)] * 4,
        in_specs=[HBM] * 4,
        out_specs=[VM] * 4,
        scratch_shapes=[pltpu.VMEM((4, 4, 2 * WIN, LANES), F32), pltpu.SemaphoreType.DMA((4,))],
        compiler_params=PARAMS,
    )(*parts)


def join_kernel(a, b, c, d, out):
    out[...] = (a[...] + b[...]) + (c[...] + d[...])


def join(parts):
    return pl.pallas_call(
        join_kernel,
        out_shape=jax.ShapeDtypeStruct((2 * WIN, LANES), F32),
        in_specs=[VM] * 4,
        out_specs=VM,
        compiler_params=PARAMS,
    )(*parts)


def dense_kernel(info, mine, got, *outs):
    me, z, r = info[0], info[1], info[2]
    ends = ends_of(info)
    first, number, _ = groups_of(ends)
    row = lax.broadcasted_iota(I32, (len(FAR) * 76, 1), 0)
    b = row + 76 * z
    for n in range(1, len(FAR)):
        b = jnp.where(row >= 76 * n, row - 76 * n + 76 * (z ^ FAR[n]), b)
    group, base = jnp.full_like(b, -1), jnp.zeros_like(b)
    for g in range(G):
        inside = (b >= first[g]) & (b < first[g] + number[g])
        group = jnp.where(inside, g, group)
        base = jnp.where(inside, first[g], base)
    window = lax.broadcasted_iota(I32, (len(FAR) * 76, WIN), 1)
    pick = (window == b - base).astype(F32).astype(BF16)
    for s in range(2):
        x = mine[WIN * s:WIN * (s + 1), :] + got[WIN * s:WIN * (s + 1), :]
        hi, mid = split(x)
        lo = ((x - hi.astype(F32)) - mid.astype(F32)).astype(BF16)
        y = jnp.dot(pick, hi, preferred_element_type=F32)
        y = y + jnp.dot(pick, mid, preferred_element_type=F32)
        y = y + jnp.dot(pick, lo, preferred_element_type=F32)
        y = jnp.where(group == lane_target(ends, info, 2 * r + s, me), y, 0.0)
        for n in range(len(FAR)):
            outs[n][76 * s:76 * (s + 1), :] = y[76 * n:76 * (n + 1), :]


def dense(info, mine, got):
    return pl.pallas_call(
        dense_kernel,
        out_shape=[jax.ShapeDtypeStruct((152, LANES), F32)] * len(FAR),
        in_specs=[SMEM, VM, VM],
        out_specs=[VM] * len(FAR),
        compiler_params=PARAMS,
    )(info, mine, got)


def halves_kernel(info, a, b, c, d, keep, give):
    r = info[2]
    x = (a[...] + b[...]) + (c[...] + d[...])
    for s in range(2):
        low, high = x[76 * s:76 * s + 38, :], x[76 * s + 38:76 * s + 76, :]
        keep[s] = jnp.where(r == 0, low, high)
        give[s] = jnp.where(r == 0, high, low)


def halves(info, parts):
    return pl.pallas_call(
        halves_kernel,
        out_shape=[jax.ShapeDtypeStruct((2, CL, LANES), F32)] * 2,
        in_specs=[SMEM] + [VM] * 4,
        out_specs=[VM] * 2,
        compiler_params=PARAMS,
    )(info, *parts)


def final_kernel(info, keep, got, out):
    r = info[2]
    for half, ref in ((r, keep), (1 - r, got)):
        for s in range(2):
            y = ref[s].T
            for i in range(IG):
                out[NC * half + IG * s + i, :, 0, :] = y[38 * i:38 * i + 38, :]


def final(info, keep, got):
    return pl.pallas_call(
        final_kernel,
        out_shape=jax.ShapeDtypeStruct((NI, CL, 1, CL), F32),
        in_specs=[SMEM, VM, VM],
        out_specs=VM,
        compiler_params=PARAMS,
    )(info, keep, got)


def swap(x, axis, step, size):
    return lax.ppermute(x, axis, [(p, p ^ step) for p in range(size)])


def exchange(parts, steps, order):
    got = [parts[0]]
    for d in order:
        pairs = [(2 * p + r, 2 * (p ^ (steps[r] * d)) + r) for p in range(PAIR) for r in range(2)]
        got.append(lax.ppermute(parts[d], ("pair", "rep"), pairs))
    return got


def per_device(amplitudes, integrals, virt_sizes, i_irrep, j_irrep):
    p, z, r = lax.axis_index("pair"), lax.axis_index("blk"), lax.axis_index("rep")
    info = jnp.concatenate([jnp.stack([p, z, r]).astype(I32), virt_sizes, i_irrep, j_irrep])
    t = jnp.swapaxes(amplitudes, 2, 3)
    other, rows = main(False, info, integrals, t)
    (own,) = main(True, info, rows, t)
    parts = add_parts(info, own, swap(other, "rep", 1, 2))
    parts = sum_parts(exchange(parts, (1, 4), (2, 3, 1)))
    x = join(exchange(parts, (4, 1), (2, 1, 3)))
    parts = dense(info, x, swap(x, "blk", 1, BLK))
    keep, give = halves(info, [parts[0]] + [swap(parts[n], "blk", FAR[n], BLK) for n in range(1, len(FAR))])
    return final(info, keep, swap(give, "rep", 1, 2))


def solution(mesh):
    return jax.shard_map(
        per_device,
        mesh=mesh,
        in_specs=(
            P(None, ("blk", "rep"), None, "pair"),
            P(("blk", "rep"), None, None, None),
            P(),
            P(),
            P(),
        ),
        out_specs=P(None, "pair", None, ("blk", "rep")),
        check_vma=False,
    )
```

```python
import functools

import jax
import jax.numpy as jnp
from jax import lax
from jax.experimental import pallas as pl
from jax.experimental.pallas import tpu as pltpu
from jax.sharding import PartitionSpec as P

NI, KL, CL, V, G = 12, 5, 38, 608, 8
PAIR, BLK = 16, 8
KP = 208
WIN = 152
SEG = 672
IG = 3
NC = NI // 2
LANES = 128
CUTS = (0, 336, 672)
WIDE = 640
FAR = (0, 3, 5, 7)
F32, BF16, I32 = jnp.float32, jnp.bfloat16, jnp.int32
SMEM = pl.BlockSpec(memory_space=pltpu.SMEM)
VM = pl.BlockSpec(memory_space=pltpu.VMEM)
HBM = pl.BlockSpec(memory_space=pltpu.HBM)
PARAMS = pltpu.CompilerParams(vmem_limit_bytes=16 * 1024 * 1024)
LARGE = pltpu.CompilerParams(vmem_limit_bytes=48 * 1024 * 1024)


def ends_of(info):
    ends, total = [], jnp.int32(0)
    for g in range(G):
        total = total + info[3 + g]
        ends.append(total)
    return ends


def groups_of(ends):
    first, number, offset = [], [], []
    last, row = jnp.int32(0), jnp.int32(0)
    for g in range(G):
        first.append(last)
        number.append(ends[g] - last)
        offset.append(row)
        row = row + ((ends[g] - last + 7) >> 3) * 8
        last = ends[g]
    return first, number, offset


def flip_of(info, i):
    return info[11 + i] ^ info[23]


def lane_target(ends, info, ig, p):
    lane = lax.broadcasted_iota(I32, (1, LANES), 1)
    second, third = lane >= 38, lane >= 76
    a = 38 * p + lane - jnp.where(third, 76, jnp.where(second, 38, 0))
    irrep = jnp.zeros((1, LANES), I32)
    for g in range(G):
        irrep = irrep + (a >= ends[g]).astype(I32)
    h = [flip_of(info, IG * ig + i) for i in range(IG)]
    h = jnp.where(third, h[2], jnp.where(second, h[1], h[0]))
    return irrep ^ h


def split(x):
    hi = x.astype(BF16)
    return hi, (x - hi.astype(F32)).astype(BF16)


def window_pick(info):
    first, number, offset = groups_of(ends_of(info))
    row = lax.broadcasted_iota(I32, (SEG, 1), 0)
    b = jnp.full((SEG, 1), -1, I32)
    for g in range(G):
        inside = (row >= offset[g]) & (row < offset[g] + number[g])
        b = jnp.where(inside, row - offset[g] + first[g], b)
    return (lax.broadcasted_iota(I32, (SEG, V), 1) == b).astype(F32).astype(BF16)


def window_rows(pick, wk, out_ref):
    hi, lo = split(wk[...])
    nt = (((1,), (1,)), ((), ()))
    wh = lax.dot_general(pick, hi, nt, preferred_element_type=F32).astype(BF16)
    wl = lax.dot_general(pick, lo, nt, preferred_element_type=F32).astype(BF16)
    out_ref[:, 0:KP] = wh
    out_ref[:, KP:2 * KP] = wh
    out_ref[:, 2 * KP:3 * KP] = wl


def main_kernel(own, info, w_in, t_hbm, out_ref, *refs):
    i0 = NC * (info[2] if own else 1 - info[2])
    if not own:
        rows_ref, raw, wk, pick, raw_sem = refs[:5]
        at = info[0] * CL
        raws = [pltpu.make_async_copy(w_in.at[k, pl.ds(at, CL)], raw.at[k], raw_sem.at[k]) for k in range(KL)]
    else:
        rows_ref, raws = w_in, []
    t_buf, x, t_all, d0, d1, in_sem = refs[-6:]
    loads = [pltpu.make_async_copy(t_hbm.at[i0 + n], t_buf.at[n], in_sem.at[n]) for n in range(NC)]
    for c in raws + loads:
        c.start()
    x[...] = jnp.zeros_like(x)
    for d in (d0, d1):
        d[SEG:, :] = jnp.zeros((WIN, 2 * LANES), F32)
    if not own:
        wk[...] = jnp.zeros_like(wk)
        pick[...] = window_pick(info)
        for c in raws:
            c.wait()
        for k in range(KL):
            wk[40 * k:40 * k + CL, :] = raw[k, :, 0, :]
        window_rows(pick[...], wk, rows_ref)
    ends = ends_of(info)
    offsets = groups_of(ends)[2]
    lane = lax.broadcasted_iota(I32, (1, WIDE), 1)
    irrep = jnp.zeros((1, WIDE), I32)
    for g in range(G):
        irrep = irrep + (lane >= ends[g]).astype(I32)

    def prepare(n):
        loads[n].wait()
        slot, odd = (n // 2) % 2, n % 2
        for k in range(KL):
            x[n % 2, 40 * k:40 * k + CL, 0:V] = t_buf[n, k]
        for c in range(5):
            tile, half = (2, odd) if c == 4 else (3 * odd + c // 2, c % 2)
            lanes = slice(half * LANES, (half + 1) * LANES)
            hi, lo = split(x[n % 2, :, c * LANES:(c + 1) * LANES])
            t_all[slot, tile, 0:KP, lanes] = hi
            t_all[slot, tile, KP:2 * KP, lanes] = lo
            t_all[slot, tile, 2 * KP:3 * KP, lanes] = hi

    def select(u, half):
        pair, tile = units[u]
        d = (d0, d1)[u % 2]
        if tile == 2:
            n, c = 2 * pair + half, 4
        else:
            n, c = 2 * pair + tile // 3, 2 * (tile % 3) + half
        target = irrep[:, c * LANES:(c + 1) * LANES] ^ flip_of(info, i0 + n)
        acc = None
        for g in range(G):
            start = pl.multiple_of(offsets[g], 8)
            part = d[pl.ds(start, WIN), half * LANES:(half + 1) * LANES]
            acc = part if g == 0 else jnp.where(target == g, part, acc)
        out_ref[n, :, c * LANES:(c + 1) * LANES] = acc

    units = [divmod(u, 5) for u in range(5 * NC // 2)]
    prepare(0)
    prepare(1)
    for u in range(len(units)):
        pair, tile = units[u]
        for half in range(2):
            rows = slice(CUTS[half], CUTS[half + 1])
            (d0, d1)[u % 2][rows, :] = jnp.dot(rows_ref[rows, :], t_all[pair % 2, tile], preferred_element_type=F32)
            if u:
                select(u - 1, half)
        if tile in (0, 2) and 2 * pair + 2 < NC:
            prepare(2 * pair + 2 + tile // 2)
    for half in range(2):
        select(len(units) - 1, half)


def main(own, info, w, t):
    packed = jax.ShapeDtypeStruct((NC, WIN, WIDE), F32)
    rows = jax.ShapeDtypeStruct((SEG, 3 * KP), BF16)
    hbm = pl.BlockSpec(memory_space=pl.ANY)
    extra = [pltpu.VMEM((KL, CL, 1, V), F32), pltpu.VMEM((KP, V), F32), pltpu.VMEM((SEG, V), BF16),
             pltpu.SemaphoreType.DMA((KL,))]
    return pl.pallas_call(
        functools.partial(main_kernel, own),
        out_shape=(packed,) if own else (packed, rows),
        in_specs=[SMEM, VM if own else hbm, hbm],
        out_specs=(VM,) if own else (VM, VM),
        scratch_shapes=([] if own else extra) + [
            pltpu.VMEM((NC, KL, CL, V), F32),
            pltpu.VMEM((2, KP, WIDE), F32),
            pltpu.VMEM((2, 5, 3 * KP, 2 * LANES), BF16),
            pltpu.VMEM((SEG + WIN, 2 * LANES), F32),
            pltpu.VMEM((SEG + WIN, 2 * LANES), F32),
            pltpu.SemaphoreType.DMA((NC,)),
        ],
        compiler_params=LARGE,
        cost_estimate=pl.CostEstimate(flops=6000000000, bytes_accessed=6000000, transcendentals=0),
    )(info, w, t)


def add_kernel(info, own_ref, got_ref, *refs):
    outs, total, tiles, sem = refs[:4], refs[4], refs[5], refs[6]
    me, r = info[0], info[2]
    copies = []
    for s in range(2):
        group, rows = slice(IG * s, IG * (s + 1)), pl.ds(WIN * s, WIN)
        total[group] = own_ref[group] + got_ref[group]
        for p in range(PAIR):
            rel = p ^ me
            low, high = rel & 3, rel >> 2
            d, u = jnp.where(r == 0, low, high), jnp.where(r == 0, high, low)
            parts = [total[IG * s + i, :, 38 * p:38 * p + 38] for i in range(IG)]
            parts.append(jnp.zeros((WIN, LANES - 38 * IG), F32))
            tiles[d, u, WIN * s:WIN * (s + 1), :] = jnp.concatenate(parts, axis=1)
        for d in range(4):
            copy = pltpu.make_async_copy(tiles.at[d, :, rows], outs[d].at[:, rows], sem.at[s, d])
            copy.start()
            copies.append(copy)
    for c in copies:
        c.wait()


def add_parts(info, own, got):
    return pl.pallas_call(
        add_kernel,
        out_shape=[jax.ShapeDtypeStruct((4, 2 * WIN, LANES), F32)] * 4,
        in_specs=[SMEM, VM, VM],
        out_specs=[HBM] * 4,
        scratch_shapes=[pltpu.VMEM(own.shape, F32), pltpu.VMEM((4, 4, 2 * WIN, LANES), F32),
                        pltpu.SemaphoreType.DMA((2, 4))],
        compiler_params=PARAMS,
        cost_estimate=pl.CostEstimate(flops=1000000, bytes_accessed=4000000, transcendentals=0),
    )(info, own, got)


def sum_kernel(*refs):
    ins, outs, buf, sem = refs[:4], refs[4:8], refs[8], refs[9]
    copies = [pltpu.make_async_copy(ins[d], buf.at[d], sem.at[d]) for d in range(4)]
    for c in copies:
        c.start()
    for c in copies:
        c.wait()
    for u in range(4):
        outs[u][...] = (buf[0, u] + buf[1, u]) + (buf[2, u] + buf[3, u])


def sum_parts(parts):
    return pl.pallas_call(
        sum_kernel,
        out_shape=[jax.ShapeDtypeStruct((2 * WIN, LANES), F32)] * 4,
        in_specs=[HBM] * 4,
        out_specs=[VM] * 4,
        scratch_shapes=[pltpu.VMEM((4, 4, 2 * WIN, LANES), F32), pltpu.SemaphoreType.DMA((4,))],
        compiler_params=PARAMS,
    )(*parts)


def join_kernel(a, b, c, d, out):
    out[...] = (a[...] + b[...]) + (c[...] + d[...])


def join(parts):
    return pl.pallas_call(
        join_kernel,
        out_shape=jax.ShapeDtypeStruct((2 * WIN, LANES), F32),
        in_specs=[VM] * 4,
        out_specs=VM,
        compiler_params=PARAMS,
    )(*parts)


def dense_kernel(info, mine, got, *outs):
    me, z, r = info[0], info[1], info[2]
    ends = ends_of(info)
    first, number, _ = groups_of(ends)
    row = lax.broadcasted_iota(I32, (len(FAR) * 76, 1), 0)
    b = row + 76 * z
    for n in range(1, len(FAR)):
        b = jnp.where(row >= 76 * n, row - 76 * n + 76 * (z ^ FAR[n]), b)
    group, base = jnp.full_like(b, -1), jnp.zeros_like(b)
    for g in range(G):
        inside = (b >= first[g]) & (b < first[g] + number[g])
        group = jnp.where(inside, g, group)
        base = jnp.where(inside, first[g], base)
    window = lax.broadcasted_iota(I32, (len(FAR) * 76, WIN), 1)
    pick = (window == b - base).astype(F32).astype(BF16)
    for s in range(2):
        x = mine[WIN * s:WIN * (s + 1), :] + got[WIN * s:WIN * (s + 1), :]
        hi, mid = split(x)
        lo = ((x - hi.astype(F32)) - mid.astype(F32)).astype(BF16)
        y = jnp.dot(pick, hi, preferred_element_type=F32)
        y = y + jnp.dot(pick, mid, preferred_element_type=F32)
        y = y + jnp.dot(pick, lo, preferred_element_type=F32)
        y = jnp.where(group == lane_target(ends, info, 2 * r + s, me), y, 0.0)
        for n in range(len(FAR)):
            outs[n][76 * s:76 * (s + 1), :] = y[76 * n:76 * (n + 1), :]


def dense(info, mine, got):
    return pl.pallas_call(
        dense_kernel,
        out_shape=[jax.ShapeDtypeStruct((152, LANES), F32)] * len(FAR),
        in_specs=[SMEM, VM, VM],
        out_specs=[VM] * len(FAR),
        compiler_params=PARAMS,
    )(info, mine, got)


def halves_kernel(info, a, b, c, d, keep, give):
    r = info[2]
    x = (a[...] + b[...]) + (c[...] + d[...])
    for s in range(2):
        low, high = x[76 * s:76 * s + 38, :], x[76 * s + 38:76 * s + 76, :]
        keep[s] = jnp.where(r == 0, low, high)
        give[s] = jnp.where(r == 0, high, low)


def halves(info, parts):
    return pl.pallas_call(
        halves_kernel,
        out_shape=[jax.ShapeDtypeStruct((2, CL, LANES), F32)] * 2,
        in_specs=[SMEM] + [VM] * 4,
        out_specs=[VM] * 2,
        compiler_params=PARAMS,
    )(info, *parts)


def final_kernel(info, keep, got, out):
    r = info[2]
    for half, ref in ((r, keep), (1 - r, got)):
        for s in range(2):
            y = ref[s].T
            for i in range(IG):
                out[NC * half + IG * s + i, :, 0, :] = y[38 * i:38 * i + 38, :]


def final(info, keep, got):
    return pl.pallas_call(
        final_kernel,
        out_shape=jax.ShapeDtypeStruct((NI, CL, 1, CL), F32),
        in_specs=[SMEM, VM, VM],
        out_specs=VM,
        compiler_params=PARAMS,
    )(info, keep, got)


def swap(x, axis, step, size):
    return lax.ppermute(x, axis, [(p, p ^ step) for p in range(size)])


def exchange(parts, steps, order):
    got = [parts[0]]
    for d in order:
        pairs = [(2 * p + r, 2 * (p ^ (steps[r] * d)) + r) for p in range(PAIR) for r in range(2)]
        got.append(lax.ppermute(parts[d], ("pair", "rep"), pairs))
    return got


def per_device(amplitudes, integrals, virt_sizes, i_irrep, j_irrep):
    p, z, r = lax.axis_index("pair"), lax.axis_index("blk"), lax.axis_index("rep")
    info = jnp.concatenate([jnp.stack([p, z, r]).astype(I32), virt_sizes, i_irrep, j_irrep])
    t = jnp.swapaxes(amplitudes, 2, 3)
    other, rows = main(False, info, integrals, t)
    (own,) = main(True, info, rows, t)
    parts = add_parts(info, own, swap(other, "rep", 1, 2))
    parts = sum_parts(exchange(parts, (1, 4), (2, 3, 1)))
    x = join(exchange(parts, (4, 1), (2, 1, 3)))
    parts = dense(info, x, swap(x, "blk", 1, BLK))
    keep, give = halves(info, [parts[0]] + [swap(parts[n], "blk", FAR[n], BLK) for n in range(1, len(FAR))])
    return final(info, keep, swap(give, "rep", 1, 2))


def solution(mesh):
    return jax.shard_map(
        per_device,
        mesh=mesh,
        in_specs=(
            P(None, ("blk", "rep"), None, "pair"),
            P(("blk", "rep"), None, None, None),
            P(),
            P(),
            P(),
        ),
        out_specs=P(None, "pair", None, ("blk", "rep")),
        check_vma=False,
    )
```

```python
import functools

import jax
import jax.numpy as jnp
from jax import lax
from jax.experimental import pallas as pl
from jax.experimental.pallas import tpu as pltpu
from jax.sharding import PartitionSpec as P

NI, KL, CL, V, G = 12, 5, 38, 608, 8
PAIR, BLK = 16, 8
KP = 208
WIN = 152
SEG = 672
IG = 3
NC = NI // 2
LANES = 128
CUTS = (0, 336, 672)
WIDE = 640
FAR = (0, 3, 5, 7)
F32, BF16, I32 = jnp.float32, jnp.bfloat16, jnp.int32
SMEM = pl.BlockSpec(memory_space=pltpu.SMEM)
VM = pl.BlockSpec(memory_space=pltpu.VMEM)
HBM = pl.BlockSpec(memory_space=pltpu.HBM)
PARAMS = pltpu.CompilerParams(vmem_limit_bytes=16 * 1024 * 1024)
LARGE = pltpu.CompilerParams(vmem_limit_bytes=48 * 1024 * 1024)


def ends_of(info):
    ends, total = [], jnp.int32(0)
    for g in range(G):
        total = total + info[3 + g]
        ends.append(total)
    return ends


def groups_of(ends):
    first, number, offset = [], [], []
    last, row = jnp.int32(0), jnp.int32(0)
    for g in range(G):
        first.append(last)
        number.append(ends[g] - last)
        offset.append(row)
        row = row + ((ends[g] - last + 7) >> 3) * 8
        last = ends[g]
    return first, number, offset


def flip_of(info, i):
    return info[11 + i] ^ info[23]


def lane_target(ends, info, ig, p):
    lane = lax.broadcasted_iota(I32, (1, LANES), 1)
    second, third = lane >= 38, lane >= 76
    a = 38 * p + lane - jnp.where(third, 76, jnp.where(second, 38, 0))
    irrep = jnp.zeros((1, LANES), I32)
    for g in range(G):
        irrep = irrep + (a >= ends[g]).astype(I32)
    h = [flip_of(info, IG * ig + i) for i in range(IG)]
    h = jnp.where(third, h[2], jnp.where(second, h[1], h[0]))
    return irrep ^ h


def split(x):
    hi = x.astype(BF16)
    return hi, (x - hi.astype(F32)).astype(BF16)


def window_pick(info):
    first, number, offset = groups_of(ends_of(info))
    row = lax.broadcasted_iota(I32, (SEG, 1), 0)
    b = jnp.full((SEG, 1), -1, I32)
    for g in range(G):
        inside = (row >= offset[g]) & (row < offset[g] + number[g])
        b = jnp.where(inside, row - offset[g] + first[g], b)
    return (lax.broadcasted_iota(I32, (SEG, V), 1) == b).astype(F32).astype(BF16)


def window_rows(pick, wk, out_ref):
    hi, lo = split(wk[...])
    nt = (((1,), (1,)), ((), ()))
    wh = lax.dot_general(pick, hi, nt, preferred_element_type=F32).astype(BF16)
    wl = lax.dot_general(pick, lo, nt, preferred_element_type=F32).astype(BF16)
    out_ref[:, 0:KP] = wh
    out_ref[:, KP:2 * KP] = wh
    out_ref[:, 2 * KP:3 * KP] = wl


def main_kernel(own, info, w_in, t_hbm, out_ref, *refs):
    i0 = NC * (info[2] if own else 1 - info[2])
    if not own:
        rows_ref, raw, wk, pick, raw_sem = refs[:5]
        at = info[0] * CL
        raws = [pltpu.make_async_copy(w_in.at[k, pl.ds(at, CL)], raw.at[k], raw_sem.at[k]) for k in range(KL)]
    else:
        rows_ref, raws = w_in, []
    t_buf, x, t_all, d0, d1, in_sem = refs[-6:]
    loads = [pltpu.make_async_copy(t_hbm.at[i0 + n], t_buf.at[n], in_sem.at[n]) for n in range(NC)]
    for c in raws + loads:
        c.start()
    x[...] = jnp.zeros_like(x)
    for d in (d0, d1):
        d[SEG:, :] = jnp.zeros((WIN, 2 * LANES), F32)
    if not own:
        wk[...] = jnp.zeros_like(wk)
        pick[...] = window_pick(info)
        for c in raws:
            c.wait()
        for k in range(KL):
            wk[40 * k:40 * k + CL, :] = raw[k, :, 0, :]
        window_rows(pick[...], wk, rows_ref)
    ends = ends_of(info)
    offsets = groups_of(ends)[2]
    lane = lax.broadcasted_iota(I32, (1, WIDE), 1)
    irrep = jnp.zeros((1, WIDE), I32)
    for g in range(G):
        irrep = irrep + (lane >= ends[g]).astype(I32)

    def prepare(n):
        loads[n].wait()
        slot, odd = (n // 2) % 2, n % 2
        for k in range(KL):
            x[n % 2, 40 * k:40 * k + CL, 0:V] = t_buf[n, k]
        for c in range(5):
            tile, half = (2, odd) if c == 4 else (3 * odd + c // 2, c % 2)
            lanes = slice(half * LANES, (half + 1) * LANES)
            hi, lo = split(x[n % 2, :, c * LANES:(c + 1) * LANES])
            t_all[slot, tile, 0:KP, lanes] = hi
            t_all[slot, tile, KP:2 * KP, lanes] = lo
            t_all[slot, tile, 2 * KP:3 * KP, lanes] = hi

    def select(u, half):
        pair, tile = units[u]
        d = (d0, d1)[u % 2]
        if tile == 2:
            n, c = 2 * pair + half, 4
        else:
            n, c = 2 * pair + tile // 3, 2 * (tile % 3) + half
        target = irrep[:, c * LANES:(c + 1) * LANES] ^ flip_of(info, i0 + n)
        acc = None
        for g in range(G):
            start = pl.multiple_of(offsets[g], 8)
            part = d[pl.ds(start, WIN), half * LANES:(half + 1) * LANES]
            acc = part if g == 0 else jnp.where(target == g, part, acc)
        out_ref[n, :, c * LANES:(c + 1) * LANES] = acc

    units = [divmod(u, 5) for u in range(5 * NC // 2)]
    prepare(0)
    prepare(1)
    for u in range(len(units)):
        pair, tile = units[u]
        for half in range(2):
            rows = slice(CUTS[half], CUTS[half + 1])
            (d0, d1)[u % 2][rows, :] = jnp.dot(rows_ref[rows, :], t_all[pair % 2, tile], preferred_element_type=F32)
            if u:
                select(u - 1, half)
        if tile in (0, 2) and 2 * pair + 2 < NC:
            prepare(2 * pair + 2 + tile // 2)
    for half in range(2):
        select(len(units) - 1, half)


def main(own, info, w, t):
    packed = jax.ShapeDtypeStruct((NC, WIN, WIDE), F32)
    rows = jax.ShapeDtypeStruct((SEG, 3 * KP), BF16)
    hbm = pl.BlockSpec(memory_space=pl.ANY)
    extra = [pltpu.VMEM((KL, CL, 1, V), F32), pltpu.VMEM((KP, V), F32), pltpu.VMEM((SEG, V), BF16),
             pltpu.SemaphoreType.DMA((KL,))]
    return pl.pallas_call(
        functools.partial(main_kernel, own),
        out_shape=(packed,) if own else (packed, rows),
        in_specs=[SMEM, VM if own else hbm, hbm],
        out_specs=(VM,) if own else (VM, VM),
        scratch_shapes=([] if own else extra) + [
            pltpu.VMEM((NC, KL, CL, V), F32),
            pltpu.VMEM((2, KP, WIDE), F32),
            pltpu.VMEM((2, 5, 3 * KP, 2 * LANES), BF16),
            pltpu.VMEM((SEG + WIN, 2 * LANES), F32),
            pltpu.VMEM((SEG + WIN, 2 * LANES), F32),
            pltpu.SemaphoreType.DMA((NC,)),
        ],
        compiler_params=LARGE,
        cost_estimate=pl.CostEstimate(flops=6000000000, bytes_accessed=6000000, transcendentals=0),
    )(info, w, t)


def add_kernel(s, info, own_ref, got_ref, *refs):
    outs, total, tiles, sem = refs[:4], refs[4], refs[5], refs[6]
    me, r = info[0], info[2]
    group = slice(IG * s, IG * (s + 1))
    total[...] = own_ref[group] + got_ref[group]
    for p in range(PAIR):
        rel = p ^ me
        low, high = rel & 3, rel >> 2
        d, u = jnp.where(r == 0, low, high), jnp.where(r == 0, high, low)
        parts = [total[i, :, 38 * p:38 * p + 38] for i in range(IG)]
        parts.append(jnp.zeros((WIN, LANES - 38 * IG), F32))
        tiles[d, u] = jnp.concatenate(parts, axis=1)
    copies = [pltpu.make_async_copy(tiles.at[d], outs[d], sem.at[d]) for d in range(4)]
    for c in copies:
        c.start()
    for c in copies:
        c.wait()


def add_parts(s, info, own, got):
    return pl.pallas_call(
        functools.partial(add_kernel, s),
        out_shape=[jax.ShapeDtypeStruct((4, WIN, LANES), F32)] * 4,
        in_specs=[SMEM, VM, VM],
        out_specs=[HBM] * 4,
        scratch_shapes=[pltpu.VMEM((IG, WIN, WIDE), F32), pltpu.VMEM((4, 4, WIN, LANES), F32),
                        pltpu.SemaphoreType.DMA((4,))],
        compiler_params=PARAMS,
        cost_estimate=pl.CostEstimate(flops=1000000, bytes_accessed=4000000, transcendentals=0),
    )(info, own, got)


def sum_kernel(*refs):
    ins, outs, buf, sem = refs[:8], refs[8:12], refs[12], refs[13]
    copies = [pltpu.make_async_copy(ins[d], buf.at[d], sem.at[d]) for d in range(8)]
    for c in copies:
        c.start()
    for s in range(2):
        for c in copies[4 * s:4 * s + 4]:
            c.wait()
        for u in range(4):
            part = [buf[4 * s + d, u] for d in range(4)]
            outs[u][WIN * s:WIN * (s + 1), :] = (part[0] + part[1]) + (part[2] + part[3])


def sum_parts(parts):
    return pl.pallas_call(
        sum_kernel,
        out_shape=[jax.ShapeDtypeStruct((2 * WIN, LANES), F32)] * 4,
        in_specs=[HBM] * 8,
        out_specs=[VM] * 4,
        scratch_shapes=[pltpu.VMEM((8, 4, WIN, LANES), F32), pltpu.SemaphoreType.DMA((8,))],
        compiler_params=PARAMS,
    )(*parts)


def join_kernel(a, b, c, d, out):
    out[...] = (a[...] + b[...]) + (c[...] + d[...])


def join(parts):
    return pl.pallas_call(
        join_kernel,
        out_shape=jax.ShapeDtypeStruct((2 * WIN, LANES), F32),
        in_specs=[VM] * 4,
        out_specs=VM,
        compiler_params=PARAMS,
    )(*parts)


def dense_kernel(info, mine, got, *outs):
    me, z, r = info[0], info[1], info[2]
    ends = ends_of(info)
    first, number, _ = groups_of(ends)
    row = lax.broadcasted_iota(I32, (len(FAR) * 76, 1), 0)
    b = row + 76 * z
    for n in range(1, len(FAR)):
        b = jnp.where(row >= 76 * n, row - 76 * n + 76 * (z ^ FAR[n]), b)
    group, base = jnp.full_like(b, -1), jnp.zeros_like(b)
    for g in range(G):
        inside = (b >= first[g]) & (b < first[g] + number[g])
        group = jnp.where(inside, g, group)
        base = jnp.where(inside, first[g], base)
    window = lax.broadcasted_iota(I32, (len(FAR) * 76, WIN), 1)
    pick = (window == b - base).astype(F32).astype(BF16)
    for s in range(2):
        x = mine[WIN * s:WIN * (s + 1), :] + got[WIN * s:WIN * (s + 1), :]
        hi, mid = split(x)
        lo = ((x - hi.astype(F32)) - mid.astype(F32)).astype(BF16)
        y = jnp.dot(pick, hi, preferred_element_type=F32)
        y = y + jnp.dot(pick, mid, preferred_element_type=F32)
        y = y + jnp.dot(pick, lo, preferred_element_type=F32)
        y = jnp.where(group == lane_target(ends, info, 2 * r + s, me), y, 0.0)
        for n in range(len(FAR)):
            outs[n][76 * s:76 * (s + 1), :] = y[76 * n:76 * (n + 1), :]


def dense(info, mine, got):
    return pl.pallas_call(
        dense_kernel,
        out_shape=[jax.ShapeDtypeStruct((152, LANES), F32)] * len(FAR),
        in_specs=[SMEM, VM, VM],
        out_specs=[VM] * len(FAR),
        compiler_params=PARAMS,
    )(info, mine, got)


def halves_kernel(info, a, b, c, d, keep, give):
    r = info[2]
    x = (a[...] + b[...]) + (c[...] + d[...])
    for s in range(2):
        low, high = x[76 * s:76 * s + 38, :], x[76 * s + 38:76 * s + 76, :]
        keep[s] = jnp.where(r == 0, low, high)
        give[s] = jnp.where(r == 0, high, low)


def halves(info, parts):
    return pl.pallas_call(
        halves_kernel,
        out_shape=[jax.ShapeDtypeStruct((2, CL, LANES), F32)] * 2,
        in_specs=[SMEM] + [VM] * 4,
        out_specs=[VM] * 2,
        compiler_params=PARAMS,
    )(info, *parts)


def final_kernel(info, keep, got, out):
    r = info[2]
    for half, ref in ((r, keep), (1 - r, got)):
        for s in range(2):
            y = ref[s].T
            for i in range(IG):
                out[NC * half + IG * s + i, :, 0, :] = y[38 * i:38 * i + 38, :]


def final(info, keep, got):
    return pl.pallas_call(
        final_kernel,
        out_shape=jax.ShapeDtypeStruct((NI, CL, 1, CL), F32),
        in_specs=[SMEM, VM, VM],
        out_specs=VM,
        compiler_params=PARAMS,
    )(info, keep, got)


def swap(x, axis, step, size):
    return lax.ppermute(x, axis, [(p, p ^ step) for p in range(size)])


def exchange(parts, steps, order):
    got = [parts[0]]
    for d in order:
        pairs = [(2 * p + r, 2 * (p ^ (steps[r] * d)) + r) for p in range(PAIR) for r in range(2)]
        got.append(lax.ppermute(parts[d], ("pair", "rep"), pairs))
    return got


def per_device(amplitudes, integrals, virt_sizes, i_irrep, j_irrep):
    p, z, r = lax.axis_index("pair"), lax.axis_index("blk"), lax.axis_index("rep")
    info = jnp.concatenate([jnp.stack([p, z, r]).astype(I32), virt_sizes, i_irrep, j_irrep])
    t = jnp.swapaxes(amplitudes, 2, 3)
    other, rows = main(False, info, integrals, t)
    (own,) = main(True, info, rows, t)
    got = swap(other, "rep", 1, 2)
    parts = [exchange(add_parts(s, info, own, got), (1, 4), (2, 3, 1)) for s in range(2)]
    parts = sum_parts(parts[0] + parts[1])
    x = join(exchange(parts, (4, 1), (2, 1, 3)))
    parts = dense(info, x, swap(x, "blk", 1, BLK))
    keep, give = halves(info, [parts[0]] + [swap(parts[n], "blk", FAR[n], BLK) for n in range(1, len(FAR))])
    return final(info, keep, swap(give, "rep", 1, 2))


def solution(mesh):
    return jax.shard_map(
        per_device,
        mesh=mesh,
        in_specs=(
            P(None, ("blk", "rep"), None, "pair"),
            P(("blk", "rep"), None, None, None),
            P(),
            P(),
            P(),
        ),
        out_specs=P(None, "pair", None, ("blk", "rep")),
        check_vma=False,
    )
```
